32 devices in a mesh: parts: 2 (over x), group: 16 (over z, y, core).
Axes of the slice: x: 2, y: 2, z: 4, core: 2. Of those that a mesh axis runs over, the one named last changes fastest.
Arguments:
- tokens: bfloat16 [4096, 2560], P(('parts', 'group')), parts along dimension 0, may hold values from -6 to 6
- routes: int32 [4096, 6], P(('parts', 'group')), parts along dimension 0, may hold values from 0 to 15, as said below
- gate_quanta: int32 [4096, 6], P(('parts', 'group')), parts along dimension 0, may hold values from 1 to 65535
- gate_weight: bfloat16 [16, 2560, 768], P('group'), may hold values from -0.125 to 0.125
- up_weight: bfloat16 [16, 2560, 768], P('group'), may hold values from -0.125 to 0.125
- down_weight: bfloat16 [16, 768, 2560], P('group'), may hold values from -0.21875 to 0.21875
Outputs:
- combined: bfloat16 [4096, 2560], P(('parts', 'group')), parts along dimension 0
The draws below stay inside these ranges and needn't reach their ends.
There are 2 independent parts, one for each index of `parts`. The reference program is written for one: setup_inputs(seed, part) draws one part's arguments, and reference() takes and returns one part's arrays. A program takes and returns all parts, laid end to end along the dimension named above; an argument that names none is the same for every part. Nothing has to cross between parts.
Inputs may be any that keep to these rules, and one draw needn't show every extreme that they name: `routes`: each row names 6 different experts, two in each of three of the 8 groups of 2 consecutive experts; among the rows of one device, at most 64 name experts of any one group, and some group is named by exactly 64 of them.
All inputs are finite; a program needn't handle non-finite values.
Results may differ from the reference program's by a relative error of at most 0.0057.
Values may be sent and summed in bfloat16 or wider, within the bound.
A program may use at most 64 MiB of HBM per device.

```python
import jax
import jax.numpy as jnp
from jax import lax

D = 2560
HID = 768
TOPK = 6
NGROUPS = 8
TOK_DEV = 128
EXPERTS = 16
EXP_GRP = 2
CAP = 64
TOKENS = 2048
N_GROUP = 16


def draw_routes(key, part):
    key = jax.random.fold_in(key, 7)
    key_order, key_columns, key_favour, key_scores = jax.random.split(key, 4)
    blocks = TOKENS // TOK_DEV
    order = jax.vmap(lambda sub: jax.random.permutation(sub, NGROUPS))(jax.random.split(key_order, blocks)).astype(jnp.int32)
    columns = jax.vmap(lambda sub: jax.random.permutation(sub, TOK_DEV))(jax.random.split(key_columns, blocks)).astype(jnp.int32)
    group_ids = jnp.arange(NGROUPS, dtype=jnp.int32)
    counts = jnp.where(group_ids < 4, TOK_DEV // 2, TOK_DEV // 4).astype(jnp.int32)
    starts = jnp.cumsum(counts) - counts
    positions = columns[:, :, None] + jnp.arange(3, dtype=jnp.int32)[None, None, :] * TOK_DEV
    place = jnp.sum((positions[:, :, :, None] >= starts[None, None, None, :]).astype(jnp.int32), axis=3) - 1
    block_ids = jnp.arange(blocks, dtype=jnp.int32)[:, None, None]
    chosen = order[block_ids, place].reshape(TOKENS, 3)
    favour = jax.random.randint(key_favour, (EXPERTS,), 0, 3) * (1 << 14)
    scores = jax.random.randint(key_scores, (TOKENS, EXPERTS), 0, 1 << 16) + favour[None, :]
    scores = scores * EXPERTS + jnp.arange(EXPERTS, dtype=jnp.int32)[None, :]
    expert_group = jnp.arange(EXPERTS, dtype=jnp.int32) // EXP_GRP
    pieces = []
    for column in range(3):
        inside = expert_group[None, :] == chosen[:, column:column + 1]
        masked = jnp.where(inside, scores, -1)
        score_top, best = lax.top_k(masked, 2)
        pieces.append(best.astype(jnp.int32))
    return jnp.concatenate(pieces, axis=1).astype(jnp.int32)


def touch_ends(array, stream_key, smallest, top_value):
    extent = array.shape
    spot = [jax.random.randint(jax.random.fold_in(stream_key, axis), (), 0, extent[axis]) for axis in range(len(extent))]
    array = array.at[tuple(spot)].set(smallest)
    longest = extent.index(max(extent))
    spot[longest] = (spot[longest] + 1) % extent[longest]
    return array.at[tuple(spot)].set(top_value)


def level_of(key, extent, cuts, low, top_value):
    loudness, own = 1.0, jax.random.fold_in(key, 6)
    for axis_at, shards_of in cuts:
        draws = jnp.exp(jax.random.uniform(jax.random.fold_in(own, axis_at), (shards_of,), jnp.float32, low / len(cuts), top_value / len(cuts)))
        loudness = loudness * jnp.repeat(draws, extent[axis_at] // shards_of).reshape([-1 if axis == axis_at else 1 for axis in range(len(extent))])
    return loudness


def gaussian(own_key, extent, scale, limit, cuts=(), kind=jnp.bfloat16):
    result = jax.random.normal(own_key, extent, jnp.float32) * scale
    if len(cuts) > 0:
        result = level_of(own_key, extent, cuts, -0.22, 0.18) * result
    return jnp.clip(result, min=-limit, max=limit).astype(kind)


def setup_inputs(seed: int = 0, part: int = 0) -> dict:
    key_of = jax.random.split(jax.random.key(seed), 7)
    part_splits = jax.random.split(jax.random.fold_in(key_of[6], part), 7)
    return {
        "tokens": gaussian(part_splits[0], (TOKENS, D), 1.0, 6.0, ((0, 16),)),
        "routes": draw_routes(jax.random.fold_in(jax.random.fold_in(key_of[6], part), 71), part),
        "gate_quanta": touch_ends(jax.random.randint(part_splits[2], (TOKENS, TOPK), 1, 65536), jax.random.fold_in(part_splits[2], 1), 1, 65535).astype(jnp.int32),
        "gate_weight": gaussian(key_of[3], (EXPERTS, D, HID), D ** -0.5, 0.125, ((0, 16),)),
        "up_weight": gaussian(key_of[4], (EXPERTS, D, HID), D ** -0.5, 0.125, ((0, 16),)),
        "down_weight": gaussian(key_of[5], (EXPERTS, HID, D), HID ** -0.5, 0.21875, ((0, 16),)),
    }


def expert_block(inputs, gate_matrix, up_matrix, down_matrix):
    gate_part = jnp.dot(inputs, gate_matrix, preferred_element_type=jnp.float32)
    up_part = jnp.dot(inputs, up_matrix, preferred_element_type=jnp.float32)
    activ = (jax.nn.silu(gate_part) * up_part).astype(jnp.bfloat16)
    return jnp.dot(activ, down_matrix, preferred_element_type=jnp.float32).astype(jnp.bfloat16)


def reference(tokens, routes, gate_quanta, gate_weight, up_weight, down_weight):
    expert_ids = jnp.arange(EXPERTS, dtype=jnp.int32)
    matches = routes[:, :, None] == expert_ids[None, None, :]
    picked = jnp.sum(matches.astype(jnp.int32), axis=1)
    gating = jnp.sum(jnp.where(matches, gate_quanta[:, :, None], 0), axis=1).astype(jnp.float32) / 65536.0
    blocked = picked.reshape(N_GROUP, TOK_DEV, EXPERTS)
    ranking = jnp.cumsum(blocked, axis=1) - blocked
    kept_mask = blocked * (ranking < CAP).astype(jnp.int32)
    slot_ids = jnp.arange(CAP, dtype=jnp.int32)
    local_ids = jnp.arange(TOK_DEV, dtype=jnp.int32)
    source_base = jnp.arange(N_GROUP, dtype=jnp.int32)[:, None] * TOK_DEV

    def one_expert(running, expert):
        kept_here = kept_mask[:, :, expert]
        rank_here = ranking[:, :, expert]
        slot_hit = (kept_here[:, :, None] == 1) & (rank_here[:, :, None] == slot_ids[None, None, :])
        position = jnp.sum(jnp.where(slot_hit, local_ids[None, :, None], 0), axis=1).astype(jnp.int32)
        present = jnp.any(slot_hit, axis=1).reshape(-1)
        token_index = (position + source_base).reshape(-1).astype(jnp.int32)
        inputs = tokens[token_index] * present[:, None].astype(tokens.dtype)
        produced = expert_block(inputs, gate_weight[expert], up_weight[expert], down_weight[expert])
        weighting = gating[token_index, expert] * present.astype(jnp.float32)
        running = running.at[token_index].add(produced.astype(jnp.float32) * weighting[:, None])
        return running, None

    running, unused = lax.scan(one_expert, jnp.zeros((TOKENS, D), jnp.float32), expert_ids)
    return running.astype(jnp.bfloat16)
```

```python
import jax
import jax.numpy as jnp
from jax import lax
from jax.experimental import pallas as pl
from jax.experimental.pallas import tpu as pltpu
from jax.sharding import PartitionSpec as P

MESH = pl.DeviceIdType.MESH
CHIPS = 8
EXTRA = 128


def flip(chip, k):
    low = lax.rem(chip + k, 2)
    mid = lax.rem(chip // 2 + k // 2, 2)
    high = lax.rem(chip // 4 + k // 4, 2)
    return high * 4 + mid * 2 + low


def paired_kernel(
    tok_ref, routes_ref, quanta_ref, gw_hbm, uw_hbm, dw_hbm, out_ref,
    gw, uw, dw, ext, slot_t, sel, outgoing, recv, activ, weight, contrib, sib, total, ret,
    w_sem, send1, recv1, send2, recv2, send3, recv3, send4, recv4,
):
    part = lax.axis_index("parts")
    me = lax.axis_index("group")
    chip, core = me // 2, lax.rem(me, 2)
    other = 1 - core
    sibling = (part, chip * 2 + other)
    tok_dev, width = tok_ref.shape
    cap = sel.shape[1]
    hid = gw.shape[1]

    loads = [
        pltpu.make_async_copy(gw_hbm.at[0], gw, w_sem.at[0]),
        pltpu.make_async_copy(uw_hbm.at[0], uw, w_sem.at[1]),
        pltpu.make_async_copy(dw_hbm.at[0], dw, w_sem.at[2]),
    ]
    for load in loads:
        load.start()

    barrier = pltpu.get_barrier_semaphore()
    for k in range(1, CHIPS):
        pl.semaphore_signal(
            barrier, inc=1, device_id=(part, flip(chip, k) * 2 + core), device_id_type=MESH
        )
    pl.semaphore_signal(barrier, inc=1, device_id=sibling, device_id_type=MESH)

    lanes = lax.broadcasted_iota(jnp.int32, (tok_dev, 128), 1)
    picked = jnp.zeros((tok_dev, 128), jnp.float32)
    quanta = jnp.zeros((tok_dev, 128), jnp.int32)
    for k in range(routes_ref.shape[1]):
        route = routes_ref[:, k : k + 1]
        picked += (route == lanes).astype(jnp.float32)
        quanta += jnp.where(
            (route == lanes) | (route == lanes - 16), quanta_ref[:, k : k + 1], 0
        )
    upper = (quanta // 256).astype(jnp.float32) / 256.0
    lower = (quanta % 256).astype(jnp.float32) / 65536.0
    ext[:, :width] = tok_ref[...]
    ext[:, width:] = jnp.where(lanes < 16, upper, lower).astype(jnp.bfloat16)
    before = (lax.broadcasted_iota(jnp.int32, (tok_dev, tok_dev), 1)
              < lax.broadcasted_iota(jnp.int32, (tok_dev, tok_dev), 0))
    ranking = jnp.dot(
        before.astype(jnp.bfloat16), picked.astype(jnp.bfloat16),
        preferred_element_type=jnp.float32,
    )
    slot_t[...] = jnp.where(picked > 0.5, ranking, -1.0).T
    slot_ids = lax.broadcasted_iota(jnp.int32, (cap, tok_dev), 0).astype(jnp.float32)

    pl.semaphore_wait(barrier, CHIPS)

    def first(k):
        return pltpu.make_async_remote_copy(
            src_ref=outgoing.at[k], dst_ref=recv.at[k, core],
            send_sem=send1.at[k], recv_sem=recv1.at[k],
            device_id=(part, flip(chip, k) * 2 + core), device_id_type=MESH)

    def share_from(src, k):
        return pltpu.make_async_remote_copy(
            src_ref=src, dst_ref=recv.at[k, core],
            send_sem=send2.at[k], recv_sem=recv2.at[k],
            device_id=sibling, device_id_type=MESH)

    def share(k):
        return share_from(recv.at[k, core], k)

    def share_in(k):
        return pltpu.make_async_remote_copy(
            src_ref=recv.at[k, other], dst_ref=recv.at[k, other],
            send_sem=send2.at[k], recv_sem=recv2.at[k],
            device_id=sibling, device_id_type=MESH)

    def cross(k):
        return pltpu.make_async_remote_copy(
            src_ref=contrib.at[k, other], dst_ref=sib.at[k],
            send_sem=send3.at[k], recv_sem=recv3.at[k],
            device_id=sibling, device_id_type=MESH)

    def back(k):
        return pltpu.make_async_remote_copy(
            src_ref=total.at[k], dst_ref=ret.at[k],
            send_sem=send4.at[k], recv_sem=recv4.at[k],
            device_id=(part, flip(chip, k) * 2 + core), device_id_type=MESH)

    def pick_rows(k):
        dest = flip(chip, k)
        chosen = (slot_t[pl.ds(2 * dest, 1), :] == slot_ids).astype(jnp.float32)
        sel[k] = chosen
        return jnp.dot(
            chosen.astype(jnp.bfloat16), ext[...], preferred_element_type=jnp.float32
        ).astype(jnp.bfloat16)

    def dispatch(j, carry):
        k = CHIPS - 1 - j
        outgoing[k] = pick_rows(k)
        first(k).start()
        return carry

    lax.fori_loop(0, CHIPS - 1, dispatch, 0)
    recv[0, core] = pick_rows(0)
    share(0).start()
    for load in loads:
        load.wait()

    rows = 4 * cap
    lane_ids = lax.broadcasted_iota(jnp.int32, (rows, EXTRA), 1)

    def expert(j, carry):
        pair = CHIPS // 2 - 1 - j
        base = 2 * pair

        def forward(k):
            first(k).wait_recv()
            share(k).start()

        forward(base + 1)

        @pl.when(base > 0)
        def _():
            forward(base)

        share_in(base + 1).wait_recv()
        share_in(base).wait_recv()

        def hidden(t, c):
            cols = pl.ds(pl.multiple_of(t * 256, 256), 256)
            x = recv[pl.ds(base, 2), :, :, :width].reshape(rows, width)
            g = jnp.dot(x, gw[:, cols], preferred_element_type=jnp.float32)
            u = jnp.dot(x, uw[:, cols], preferred_element_type=jnp.float32)
            activ[:, cols] = (g / (1.0 + jnp.exp(-g)) * u).astype(jnp.bfloat16)
            return c

        lax.fori_loop(0, hid // 256, hidden, 0)
        marks = recv[pl.ds(base, 2), :, :, width:].reshape(rows, EXTRA).astype(jnp.float32)
        mine = (lane_ids == me) | (lane_ids == me + 16)
        weight[...] = jnp.broadcast_to(
            jnp.sum(jnp.where(mine, marks, 0.0), axis=1, keepdims=True), (rows, 128))

        def down(t, c):
            cols = pl.ds(pl.multiple_of(t * 512, 512), 512)
            o = jnp.dot(activ[...], dw[:, cols], preferred_element_type=jnp.float32)
            o = o * weight[:, :1]
            contrib[pl.ds(base, 2), :, :, cols] = o.astype(jnp.bfloat16).reshape(2, 2, cap, 512)
            return c

        lax.fori_loop(0, width // 512, down, 0)
        cross(base + 1).start()
        cross(base).start()

        def finish(k):
            cross(k).wait_recv()
            return (
                contrib[k, core].astype(jnp.float32) + sib[k].astype(jnp.float32)
            ).astype(jnp.bfloat16)

        total[base + 1] = finish(base + 1)
        back(base + 1).start()

        @pl.when(base > 0)
        def _():
            total[base] = finish(base)
            back(base).start()

        @pl.when(base == 0)
        def _():
            ret[0] = finish(0)

        return carry

    lax.fori_loop(0, CHIPS // 2, expert, 0)

    def arrive(j, carry):
        back(CHIPS - 1 - j).wait_recv()
        return carry

    lax.fori_loop(0, CHIPS - 1, arrive, 0)
    spread = sel[...].reshape(CHIPS * cap, tok_dev).T.astype(jnp.bfloat16)

    def gather(t, c):
        cols = pl.ds(pl.multiple_of(t * 512, 512), 512)
        got = ret[:, :, cols].reshape(CHIPS * cap, 512)
        out_ref[:, cols] = jnp.dot(
            spread, got, preferred_element_type=jnp.float32
        ).astype(out_ref.dtype)
        return c

    lax.fori_loop(0, width // 512, gather, 0)

    def drain(k, carry):
        first(k).wait_send()
        back(k).wait_send()
        return carry

    lax.fori_loop(1, CHIPS, drain, 0)

    def drain_sibling(k, carry):
        share(k).wait_send()
        cross(k).wait_send()
        return carry

    lax.fori_loop(0, CHIPS, drain_sibling, 0)


def paired_body(tokens, routes, gate_quanta, gate_weight, up_weight, down_weight):
    tok_dev, width = tokens.shape
    experts = lax.axis_size("group")
    cap = 4 * tok_dev * routes.shape[1] // (3 * experts)
    hid = gate_weight.shape[2]
    bf, f32 = jnp.bfloat16, jnp.float32
    dma = pltpu.SemaphoreType.DMA
    vmem = pl.BlockSpec(memory_space=pltpu.VMEM)
    hbm = pl.BlockSpec(memory_space=pl.ANY)
    return pl.pallas_call(
        paired_kernel,
        out_shape=jax.ShapeDtypeStruct((tok_dev, width), bf),
        in_specs=[vmem, vmem, vmem, hbm, hbm, hbm],
        out_specs=vmem,
        scratch_shapes=[
            pltpu.VMEM((width, hid), bf),
            pltpu.VMEM((width, hid), bf),
            pltpu.VMEM((hid, width), bf),
            pltpu.VMEM((tok_dev, width + EXTRA), bf),
            pltpu.VMEM((128, tok_dev), f32),
            pltpu.VMEM((CHIPS, cap, tok_dev), f32),
            pltpu.VMEM((CHIPS, cap, width + EXTRA), bf),
            pltpu.VMEM((CHIPS, 2, cap, width + EXTRA), bf),
            pltpu.VMEM((4 * cap, hid), bf),
            pltpu.VMEM((4 * cap, 128), f32),
            pltpu.VMEM((CHIPS, 2, cap, width), bf),
            pltpu.VMEM((CHIPS, cap, width), bf),
            pltpu.VMEM((CHIPS, cap, width), bf),
            pltpu.VMEM((CHIPS, cap, width), bf),
            dma((3,)),
        ] + [dma((CHIPS,))] * 8,
        compiler_params=pltpu.CompilerParams(
            collective_id=0, has_side_effects=True, vmem_limit_bytes=52 * 1024 * 1024
        ),
        cost_estimate=pl.CostEstimate(
            flops=6 * 16 * cap * width * hid, bytes_accessed=6 * width * hid, transcendentals=0
        ),
    )(tokens, routes, gate_quanta, gate_weight, up_weight, down_weight)


def expert_apply(received, gate_weight, up_weight, down_weight):
    senders = received.shape[0]
    slots_here = received.shape[1]
    inputs = received.reshape(senders * slots_here, received.shape[2])
    gate_part = jnp.dot(inputs, gate_weight[0], preferred_element_type=jnp.float32)
    up_part = jnp.dot(inputs, up_weight[0], preferred_element_type=jnp.float32)
    activ = (jax.nn.silu(gate_part) * up_part).astype(jnp.bfloat16)
    produced = jnp.dot(activ, down_weight[0], preferred_element_type=jnp.float32).astype(
        jnp.bfloat16
    )
    return produced.reshape(senders, slots_here, produced.shape[1])


def body(tokens, routes, gate_quanta, gate_weight, up_weight, down_weight):
    experts = lax.axis_size("group")
    tok_dev = tokens.shape[0]
    width = tokens.shape[1]
    topk = routes.shape[1]
    capacity = 4 * tok_dev * topk // (3 * experts)
    expert_ids = jnp.arange(experts, dtype=jnp.int32)
    matches = routes[:, :, None] == expert_ids[None, None, :]
    picked = jnp.sum(matches.astype(jnp.int32), axis=1)
    weight_quanta = jnp.sum(jnp.where(matches, gate_quanta[:, :, None], 0), axis=1)
    ranking = jnp.cumsum(picked, axis=0) - picked
    slot_of = jnp.where((picked == 1) & (ranking < capacity), ranking, -1)
    contract = (((0,), (0,)), ((), ()))
    selector = slot_of.T[:, None, :] == jnp.arange(capacity, dtype=jnp.int32)[None, :, None]
    selector_float = selector.astype(jnp.float32)
    selector_bf = selector.astype(jnp.bfloat16).reshape(experts * capacity, tok_dev)
    outgoing = jnp.dot(selector_bf, tokens, preferred_element_type=jnp.float32).astype(jnp.bfloat16)
    outgoing = outgoing.reshape(experts, capacity, width)
    produced = expert_apply(
        lax.all_to_all(outgoing, "group", split_axis=0, concat_axis=0, tiled=True),
        gate_weight,
        up_weight,
        down_weight,
    )
    returned = lax.all_to_all(produced, "group", split_axis=0, concat_axis=0, tiled=True)
    upper_part = (weight_quanta // 256).astype(jnp.float32).T / 256.0
    lower_part = (weight_quanta % 256).astype(jnp.float32).T / 65536.0
    combine_upper = (
        (selector_float * upper_part[:, None, :])
        .astype(jnp.bfloat16)
        .reshape(experts * capacity, tok_dev)
    )
    combine_lower = (
        (selector_float * lower_part[:, None, :])
        .astype(jnp.bfloat16)
        .reshape(experts * capacity, tok_dev)
    )
    flat_rows = returned.reshape(experts * capacity, width)
    running = lax.dot_general(
        combine_upper, flat_rows, contract, preferred_element_type=jnp.float32
    )
    running = running + lax.dot_general(
        combine_lower, flat_rows, contract, preferred_element_type=jnp.float32
    )
    return running.astype(jnp.bfloat16)


def solution(mesh):
    placed = (
        P(("parts", "group"), None),
        P(("parts", "group"), None),
        P(("parts", "group"), None),
        P("group", None, None),
        P("group", None, None),
        P("group", None, None),
    )
    chosen = paired_body if mesh.shape["group"] == 2 * CHIPS else body
    return jax.shard_map(
        chosen, mesh=mesh, in_specs=placed, out_specs=P(("parts", "group"), None), check_vma=False
    )
```

```python
import jax
import jax.numpy as jnp
from jax import lax
from jax.experimental import pallas as pl
from jax.experimental.pallas import tpu as pltpu
from jax.sharding import PartitionSpec as P

MESH = pl.DeviceIdType.MESH
CHIPS = 8
HALF = CHIPS // 2
EXTRA = 128


def flip(chip, k):
    low = lax.rem(chip + k, 2)
    mid = lax.rem(chip // 2 + k // 2, 2)
    high = lax.rem(chip // 4 + k // 4, 2)
    return high * 4 + mid * 2 + low


def paired_kernel(
    tok_ref, routes_ref, quanta_ref, gw_hbm, uw_hbm, dw_hbm, out_ref,
    gw, uw, dw, ext, slot_t, sel, outgoing, recv, activ, weight, contrib, sib, total, ret,
    partial, landed, w_sem, block_send, block_recv, part_send, part_recv, send1, recv1, send2, recv2, send3, recv3, send4, recv4,
):
    part = lax.axis_index("parts")
    me = lax.axis_index("group")
    chip, core = me // 2, lax.rem(me, 2)
    other = 1 - core
    sibling = (part, chip * 2 + other)
    tok_dev, width = tok_ref.shape
    cap = sel.shape[1]
    hid = gw.shape[1]

    loads = [
        pltpu.make_async_copy(gw_hbm.at[0], gw, w_sem.at[0]),
        pltpu.make_async_copy(uw_hbm.at[0], uw, w_sem.at[1]),
        pltpu.make_async_copy(dw_hbm.at[0], dw, w_sem.at[2]),
    ]
    for load in loads:
        load.start()

    barrier = pltpu.get_barrier_semaphore()
    for k in range(1, HALF + 1):
        pl.semaphore_signal(
            barrier, inc=1, device_id=(part, flip(chip, k) * 2 + core), device_id_type=MESH
        )
    pl.semaphore_signal(barrier, inc=1, device_id=sibling, device_id_type=MESH)

    lanes = lax.broadcasted_iota(jnp.int32, (tok_dev, 128), 1)
    picked = jnp.zeros((tok_dev, 128), jnp.float32)
    quanta = jnp.zeros((tok_dev, 128), jnp.int32)
    for k in range(routes_ref.shape[1]):
        route = routes_ref[:, k : k + 1]
        picked += (route == lanes).astype(jnp.float32)
        quanta += jnp.where(
            (route == lanes) | (route == lanes - 16), quanta_ref[:, k : k + 1], 0
        )
    upper = (quanta // 256).astype(jnp.float32) / 256.0
    lower = (quanta % 256).astype(jnp.float32) / 65536.0
    before = (lax.broadcasted_iota(jnp.int32, (tok_dev, tok_dev), 1)
              < lax.broadcasted_iota(jnp.int32, (tok_dev, tok_dev), 0))
    ranking = jnp.dot(
        before.astype(jnp.bfloat16), picked.astype(jnp.bfloat16),
        preferred_element_type=jnp.float32,
    )
    slots = jnp.where(picked > 0.5, ranking, -1.0)
    slot_t[0] = slots.T
    ext[0, :, :width] = tok_ref[...]
    marks = jnp.where(lanes < 16, upper, lower)
    ext[0, :, width : width + EXTRA] = marks.astype(jnp.bfloat16)
    ext[0, :, width + EXTRA :] = slots.astype(jnp.bfloat16)
    slot_ids = lax.broadcasted_iota(jnp.int32, (cap, tok_dev), 0).astype(jnp.float32)

    pl.semaphore_wait(barrier, HALF + 1)

    mirror = (part, flip(chip, HALF) * 2 + core)
    block = pltpu.make_async_remote_copy(
        src_ref=ext.at[0], dst_ref=ext.at[1],
        send_sem=block_send.at[0], recv_sem=block_recv.at[0],
        device_id=mirror, device_id_type=MESH)
    block.start()

    def first(k):
        return pltpu.make_async_remote_copy(
            src_ref=outgoing.at[k], dst_ref=recv.at[k, core],
            send_sem=send1.at[k], recv_sem=recv1.at[k],
            device_id=(part, flip(chip, lax.rem(k, HALF)) * 2 + core), device_id_type=MESH)

    def share_from(src, k):
        return pltpu.make_async_remote_copy(
            src_ref=src, dst_ref=recv.at[k, core],
            send_sem=send2.at[k], recv_sem=recv2.at[k],
            device_id=sibling, device_id_type=MESH)

    def share(k):
        return share_from(recv.at[k, core], k)

    def share_in(k):
        return pltpu.make_async_remote_copy(
            src_ref=recv.at[k, other], dst_ref=recv.at[k, other],
            send_sem=send2.at[k], recv_sem=recv2.at[k],
            device_id=sibling, device_id_type=MESH)

    def cross(k):
        return pltpu.make_async_remote_copy(
            src_ref=contrib.at[k, other], dst_ref=sib.at[k],
            send_sem=send3.at[k], recv_sem=recv3.at[k],
            device_id=sibling, device_id_type=MESH)

    def back(k):
        return pltpu.make_async_remote_copy(
            src_ref=total.at[k], dst_ref=ret.at[k],
            send_sem=send4.at[k], recv_sem=recv4.at[k],
            device_id=(part, flip(chip, lax.rem(k, HALF)) * 2 + core), device_id_type=MESH)

    def sum_piece(h):
        return pltpu.make_async_remote_copy(
            src_ref=partial.at[h], dst_ref=landed.at[h],
            send_sem=part_send.at[h], recv_sem=part_recv.at[h],
            device_id=mirror, device_id_type=MESH)

    def pick_rows(k):
        dest = flip(chip, lax.rem(k, HALF))
        held = k // HALF
        chosen = (slot_t[held, pl.ds(2 * dest, 1), :] == slot_ids).astype(jnp.float32)
        sel[k] = chosen
        return jnp.dot(
            chosen.astype(jnp.bfloat16), ext[held, :, : width + EXTRA],
            preferred_element_type=jnp.float32,
        ).astype(jnp.bfloat16)

    def dispatch(k, carry):
        outgoing[k] = pick_rows(k)
        first(k).start()
        return carry

    lax.fori_loop(1, HALF, dispatch, 0)
    recv[0, core] = pick_rows(0)
    share(0).start()
    for load in loads:
        load.wait()

    rows = 4 * cap
    lane_ids = lax.broadcasted_iota(jnp.int32, (rows, EXTRA), 1)

    def expert(pair, far):
        base = 2 * pair
        local = 4 if far else 0

        def forward(k):
            first(k).wait_recv()
            share(k).start()

        forward(base + 1)

        @pl.when(base != local)
        def _():
            forward(base)

        share_in(base + 1).wait_recv()
        share_in(base).wait_recv()

        def hidden(t, c):
            cols = pl.ds(pl.multiple_of(t * 256, 256), 256)
            x = recv[pl.ds(base, 2), :, :, :width].reshape(rows, width)
            g = jnp.dot(x, gw[:, cols], preferred_element_type=jnp.float32)
            u = jnp.dot(x, uw[:, cols], preferred_element_type=jnp.float32)
            activ[:, cols] = (g / (1.0 + jnp.exp(-g)) * u).astype(jnp.bfloat16)
            return c

        lax.fori_loop(0, hid // 256, hidden, 0)
        marks = recv[pl.ds(base, 2), :, :, width:].reshape(rows, EXTRA).astype(jnp.float32)
        mine = (lane_ids == me) | (lane_ids == me + 16)
        weight[...] = jnp.broadcast_to(
            jnp.sum(jnp.where(mine, marks, 0.0), axis=1, keepdims=True), (rows, 128))

        def down(t, c):
            cols = pl.ds(pl.multiple_of(t * 512, 512), 512)
            o = jnp.dot(activ[...], dw[:, cols], preferred_element_type=jnp.float32)
            o = o * weight[:, :1]
            contrib[pl.ds(base, 2), :, :, cols] = o.astype(jnp.bfloat16).reshape(2, 2, cap, 512)
            return c

        lax.fori_loop(0, width // 512, down, 0)
        cross(base + 1).start()
        cross(base).start()

        def finish(k):
            cross(k).wait_recv()
            return (
                contrib[k, core].astype(jnp.float32) + sib[k].astype(jnp.float32)
            ).astype(jnp.bfloat16)

        total[base + 1] = finish(base + 1)
        if far:
            back(base + 1).start()

        @pl.when(base != local)
        def _():
            total[base] = finish(base)
            if far:
                back(base).start()

        @pl.when(base == local)
        def _():
            ret[local] = finish(local)

    def near_pair(pair, carry):
        expert(pair, False)
        return carry

    def far_pair(pair, carry):
        expert(pair, True)
        return carry

    lax.fori_loop(0, 2, near_pair, 0)

    block.wait_recv()
    slot_t[1] = ext[1, :, width + EXTRA :].astype(jnp.float32).T
    lax.fori_loop(HALF + 1, CHIPS, dispatch, 0)
    recv[HALF, core] = pick_rows(HALF)
    share(HALF).start()
    lax.fori_loop(2, 4, far_pair, 0)

    def arrive(k, carry):
        back(k).wait_recv()
        return carry

    def send_back(k, carry):
        back(k).start()
        return carry

    half_width = width // 2
    span = half_width // 5

    def spread_of(lo):
        return sel[lo : lo + HALF].reshape(HALF * cap, tok_dev).T.astype(jnp.bfloat16)

    lax.fori_loop(HALF + 1, CHIPS, arrive, 0)
    spread_far = spread_of(HALF)
    for h in range(2):
        def add_far(t, c):
            cols = pl.ds(pl.multiple_of(h * half_width + t * span, span), span)
            got = ret[HALF:, :, cols].reshape(HALF * cap, span)
            into = pl.ds(pl.multiple_of(t * span, span), span)
            partial[h, :, into] = jnp.dot(
                spread_far, got, preferred_element_type=jnp.float32
            ).astype(jnp.bfloat16)
            return c

        lax.fori_loop(0, 5, add_far, 0)
        sum_piece(h).start()

    lax.fori_loop(1, HALF, send_back, 0)
    lax.fori_loop(1, HALF, arrive, 0)
    spread_near = spread_of(0)
    for h in range(2):
        sum_piece(h).wait_recv()

        def gather(t, c):
            cols = pl.ds(pl.multiple_of(h * half_width + t * span, span), span)
            got = ret[:HALF, :, cols].reshape(HALF * cap, span)
            from_far = landed[h, :, pl.ds(pl.multiple_of(t * span, span), span)]
            out_ref[:, cols] = (
                jnp.dot(spread_near, got, preferred_element_type=jnp.float32)
                + from_far.astype(jnp.float32)
            ).astype(out_ref.dtype)
            return c

        lax.fori_loop(0, 5, gather, 0)

    block.wait_send()
    for h in range(2):
        sum_piece(h).wait_send()

    def drain(k, carry):
        first(k).wait_send()
        back(k).wait_send()
        return carry

    lax.fori_loop(1, HALF, drain, 0)
    lax.fori_loop(HALF + 1, CHIPS, drain, 0)

    def drain_sibling(k, carry):
        share(k).wait_send()
        cross(k).wait_send()
        return carry

    lax.fori_loop(0, CHIPS, drain_sibling, 0)


def paired_body(tokens, routes, gate_quanta, gate_weight, up_weight, down_weight):
    tok_dev, width = tokens.shape
    experts = lax.axis_size("group")
    cap = 4 * tok_dev * routes.shape[1] // (3 * experts)
    hid = gate_weight.shape[2]
    bf, f32 = jnp.bfloat16, jnp.float32
    dma = pltpu.SemaphoreType.DMA
    vmem = pl.BlockSpec(memory_space=pltpu.VMEM)
    hbm = pl.BlockSpec(memory_space=pl.ANY)
    return pl.pallas_call(
        paired_kernel,
        out_shape=jax.ShapeDtypeStruct((tok_dev, width), bf),
        in_specs=[vmem, vmem, vmem, hbm, hbm, hbm],
        out_specs=vmem,
        scratch_shapes=[
            pltpu.VMEM((width, hid), bf),
            pltpu.VMEM((width, hid), bf),
            pltpu.VMEM((hid, width), bf),
            pltpu.VMEM((2, tok_dev, width + 2 * EXTRA), bf),
            pltpu.VMEM((2, 128, tok_dev), f32),
            pltpu.VMEM((CHIPS, cap, tok_dev), f32),
            pltpu.VMEM((CHIPS, cap, width + EXTRA), bf),
            pltpu.VMEM((CHIPS, 2, cap, width + EXTRA), bf),
            pltpu.VMEM((4 * cap, hid), bf),
            pltpu.VMEM((4 * cap, 128), f32),
            pltpu.VMEM((CHIPS, 2, cap, width), bf),
            pltpu.VMEM((CHIPS, cap, width), bf),
            pltpu.VMEM((CHIPS, cap, width), bf),
            pltpu.VMEM((CHIPS, cap, width), bf),
            pltpu.VMEM((2, tok_dev, width // 2), bf),
            pltpu.VMEM((2, tok_dev, width // 2), bf),
            dma((3,)),
            dma((1,)), dma((1,)), dma((2,)), dma((2,)),
        ] + [dma((CHIPS,))] * 8,
        compiler_params=pltpu.CompilerParams(
            collective_id=0, has_side_effects=True, vmem_limit_bytes=52 * 1024 * 1024
        ),
        cost_estimate=pl.CostEstimate(
            flops=6 * 16 * cap * width * hid, bytes_accessed=6 * width * hid, transcendentals=0
        ),
    )(tokens, routes, gate_quanta, gate_weight, up_weight, down_weight)


def expert_apply(received, gate_weight, up_weight, down_weight):
    senders = received.shape[0]
    slots_here = received.shape[1]
    inputs = received.reshape(senders * slots_here, received.shape[2])
    gate_part = jnp.dot(inputs, gate_weight[0], preferred_element_type=jnp.float32)
    up_part = jnp.dot(inputs, up_weight[0], preferred_element_type=jnp.float32)
    activ = (jax.nn.silu(gate_part) * up_part).astype(jnp.bfloat16)
    produced = jnp.dot(activ, down_weight[0], preferred_element_type=jnp.float32).astype(
        jnp.bfloat16
    )
    return produced.reshape(senders, slots_here, produced.shape[1])


def body(tokens, routes, gate_quanta, gate_weight, up_weight, down_weight):
    experts = lax.axis_size("group")
    tok_dev = tokens.shape[0]
    width = tokens.shape[1]
    topk = routes.shape[1]
    capacity = 4 * tok_dev * topk // (3 * experts)
    expert_ids = jnp.arange(experts, dtype=jnp.int32)
    matches = routes[:, :, None] == expert_ids[None, None, :]
    picked = jnp.sum(matches.astype(jnp.int32), axis=1)
    weight_quanta = jnp.sum(jnp.where(matches, gate_quanta[:, :, None], 0), axis=1)
    ranking = jnp.cumsum(picked, axis=0) - picked
    slot_of = jnp.where((picked == 1) & (ranking < capacity), ranking, -1)
    contract = (((0,), (0,)), ((), ()))
    selector = slot_of.T[:, None, :] == jnp.arange(capacity, dtype=jnp.int32)[None, :, None]
    selector_float = selector.astype(jnp.float32)
    selector_bf = selector.astype(jnp.bfloat16).reshape(experts * capacity, tok_dev)
    outgoing = jnp.dot(selector_bf, tokens, preferred_element_type=jnp.float32).astype(jnp.bfloat16)
    outgoing = outgoing.reshape(experts, capacity, width)
    produced = expert_apply(
        lax.all_to_all(outgoing, "group", split_axis=0, concat_axis=0, tiled=True),
        gate_weight,
        up_weight,
        down_weight,
    )
    returned = lax.all_to_all(produced, "group", split_axis=0, concat_axis=0, tiled=True)
    upper_part = (weight_quanta // 256).astype(jnp.float32).T / 256.0
    lower_part = (weight_quanta % 256).astype(jnp.float32).T / 65536.0
    combine_upper = (
        (selector_float * upper_part[:, None, :])
        .astype(jnp.bfloat16)
        .reshape(experts * capacity, tok_dev)
    )
    combine_lower = (
        (selector_float * lower_part[:, None, :])
        .astype(jnp.bfloat16)
        .reshape(experts * capacity, tok_dev)
    )
    flat_rows = returned.reshape(experts * capacity, width)
    running = lax.dot_general(
        combine_upper, flat_rows, contract, preferred_element_type=jnp.float32
    )
    running = running + lax.dot_general(
        combine_lower, flat_rows, contract, preferred_element_type=jnp.float32
    )
    return running.astype(jnp.bfloat16)


def solution(mesh):
    placed = (
        P(("parts", "group"), None),
        P(("parts", "group"), None),
        P(("parts", "group"), None),
        P("group", None, None),
        P("group", None, None),
        P("group", None, None),
    )
    chosen = paired_body if mesh.shape["group"] == 2 * CHIPS else body
    return jax.shard_map(
        chosen, mesh=mesh, in_specs=placed, out_specs=P(("parts", "group"), None), check_vma=False
    )
```

```python
import jax
import jax.numpy as jnp
from jax import lax
from jax.experimental import pallas as pl
from jax.experimental.pallas import tpu as pltpu
from jax.sharding import PartitionSpec as P

MESH = pl.DeviceIdType.MESH
CHIPS = 8
HALF = CHIPS // 2
EXTRA = 128


def flip(chip, k):
    low = lax.rem(chip + k, 2)
    mid = lax.rem(chip // 2 + k // 2, 2)
    high = lax.rem(chip // 4 + k // 4, 2)
    return high * 4 + mid * 2 + low


def paired_kernel(
    tok_ref, routes_ref, quanta_ref, gw_hbm, uw_hbm, dw_hbm, out_ref,
    gw, uw, dw, ext, slot_t, sel, outgoing, recv, activ, weight, contrib, sib, total, ret,
    partial, landed, w_sem, block_send, block_recv, part_send, part_recv, send1, recv1, send2, recv2, send3, recv3, send4, recv4,
):
    part = lax.axis_index("parts")
    me = lax.axis_index("group")
    chip, core = me // 2, lax.rem(me, 2)
    other = 1 - core
    sibling = (part, chip * 2 + other)
    tok_dev, width = tok_ref.shape
    cap = sel.shape[1]
    hid = gw.shape[1]

    loads = [
        pltpu.make_async_copy(gw_hbm.at[0], gw, w_sem.at[0]),
        pltpu.make_async_copy(uw_hbm.at[0], uw, w_sem.at[1]),
        pltpu.make_async_copy(dw_hbm.at[0], dw, w_sem.at[2]),
    ]
    for load in loads:
        load.start()

    barrier = pltpu.get_barrier_semaphore()
    for k in range(1, HALF + 1):
        pl.semaphore_signal(
            barrier, inc=1, device_id=(part, flip(chip, k) * 2 + core), device_id_type=MESH
        )
    pl.semaphore_signal(barrier, inc=1, device_id=sibling, device_id_type=MESH)

    lanes = lax.broadcasted_iota(jnp.int32, (tok_dev, 128), 1)
    picked = jnp.zeros((tok_dev, 128), jnp.float32)
    quanta = jnp.zeros((tok_dev, 128), jnp.int32)
    for k in range(routes_ref.shape[1]):
        route = routes_ref[:, k : k + 1]
        picked += (route == lanes).astype(jnp.float32)
        quanta += jnp.where(
            (route == lanes) | (route == lanes - 16), quanta_ref[:, k : k + 1], 0
        )
    upper = (quanta // 256).astype(jnp.float32) / 256.0
    lower = (quanta % 256).astype(jnp.float32) / 65536.0
    before = (lax.broadcasted_iota(jnp.int32, (tok_dev, tok_dev), 1)
              < lax.broadcasted_iota(jnp.int32, (tok_dev, tok_dev), 0))
    ranking = jnp.dot(
        before.astype(jnp.bfloat16), picked.astype(jnp.bfloat16),
        preferred_element_type=jnp.float32,
    )
    slots = jnp.where(picked > 0.5, ranking, -1.0)
    slot_t[0] = slots.T
    ext[0, :, :width] = tok_ref[...]
    marks = jnp.where(lanes < 16, upper, lower)
    ext[0, :, width : width + EXTRA] = marks.astype(jnp.bfloat16)
    ext[0, :, width + EXTRA :] = slots.astype(jnp.bfloat16)
    slot_ids = lax.broadcasted_iota(jnp.int32, (cap, tok_dev), 0).astype(jnp.float32)

    pl.semaphore_wait(barrier, HALF + 1)

    mirror = (part, flip(chip, HALF) * 2 + core)
    block = pltpu.make_async_remote_copy(
        src_ref=ext.at[0], dst_ref=ext.at[1],
        send_sem=block_send.at[0], recv_sem=block_recv.at[0],
        device_id=mirror, device_id_type=MESH)
    block.start()

    def first(k):
        return pltpu.make_async_remote_copy(
            src_ref=outgoing.at[k], dst_ref=recv.at[k, core],
            send_sem=send1.at[k], recv_sem=recv1.at[k],
            device_id=(part, flip(chip, lax.rem(k, HALF)) * 2 + core), device_id_type=MESH)

    def share_from(src, k):
        return pltpu.make_async_remote_copy(
            src_ref=src, dst_ref=recv.at[k, core],
            send_sem=send2.at[k], recv_sem=recv2.at[k],
            device_id=sibling, device_id_type=MESH)

    def share(k):
        return share_from(recv.at[k, core], k)

    def share_in(k):
        return pltpu.make_async_remote_copy(
            src_ref=recv.at[k, other], dst_ref=recv.at[k, other],
            send_sem=send2.at[k], recv_sem=recv2.at[k],
            device_id=sibling, device_id_type=MESH)

    def cross(k):
        return pltpu.make_async_remote_copy(
            src_ref=contrib.at[k, other], dst_ref=sib.at[k],
            send_sem=send3.at[k], recv_sem=recv3.at[k],
            device_id=sibling, device_id_type=MESH)

    def back(k):
        return pltpu.make_async_remote_copy(
            src_ref=total.at[k], dst_ref=ret.at[k],
            send_sem=send4.at[k], recv_sem=recv4.at[k],
            device_id=(part, flip(chip, lax.rem(k, HALF)) * 2 + core), device_id_type=MESH)

    def sum_piece(h):
        return pltpu.make_async_remote_copy(
            src_ref=partial.at[h], dst_ref=landed.at[h],
            send_sem=part_send.at[h], recv_sem=part_recv.at[h],
            device_id=mirror, device_id_type=MESH)

    def pick_rows(k):
        dest = flip(chip, lax.rem(k, HALF))
        held = k // HALF
        chosen = (slot_t[held, pl.ds(2 * dest, 1), :] == slot_ids).astype(jnp.float32)
        sel[k] = chosen
        return jnp.dot(
            chosen.astype(jnp.bfloat16), ext[held, :, : width + EXTRA],
            preferred_element_type=jnp.float32,
        ).astype(jnp.bfloat16)

    def dispatch(k, carry):
        outgoing[k] = pick_rows(k)
        first(k).start()
        return carry

    lax.fori_loop(1, HALF, dispatch, 0)
    recv[0, core] = pick_rows(0)
    share(0).start()
    rows = 4 * cap
    lane_ids = lax.broadcasted_iota(jnp.int32, (rows, EXTRA), 1)

    def expert(pair, far):
        base = 2 * pair
        local = 4 if far else 0

        def forward(k):
            first(k).wait_recv()
            share(k).start()

        forward(base + 1)

        @pl.when(base != local)
        def _():
            forward(base)

        share_in(base + 1).wait_recv()
        share_in(base).wait_recv()

        def hidden(t, c):
            cols = pl.ds(pl.multiple_of(t * 256, 256), 256)
            x = recv[pl.ds(base, 2), :, :, :width].reshape(rows, width)
            g = jnp.dot(x, gw[:, cols], preferred_element_type=jnp.float32)
            u = jnp.dot(x, uw[:, cols], preferred_element_type=jnp.float32)
            activ[:, cols] = (g / (1.0 + jnp.exp(-g)) * u).astype(jnp.bfloat16)
            return c

        lax.fori_loop(0, hid // 256, hidden, 0)
        marks = recv[pl.ds(base, 2), :, :, width:].reshape(rows, EXTRA).astype(jnp.float32)
        mine = (lane_ids == me) | (lane_ids == me + 16)
        weight[...] = jnp.broadcast_to(
            jnp.sum(jnp.where(mine, marks, 0.0), axis=1, keepdims=True), (rows, 128))

        def down(t, c):
            cols = pl.ds(pl.multiple_of(t * 512, 512), 512)
            o = jnp.dot(activ[...], dw[:, cols], preferred_element_type=jnp.float32)
            o = o * weight[:, :1]
            contrib[pl.ds(base, 2), :, :, cols] = o.astype(jnp.bfloat16).reshape(2, 2, cap, 512)
            return c

        lax.fori_loop(0, width // 512, down, 0)
        cross(base + 1).start()
        cross(base).start()
        if far:
            finish(base + 1)
            finish(base)

    def finish(k):
        cross(k).wait_recv()
        both = (
            contrib[k, core].astype(jnp.float32) + sib[k].astype(jnp.float32)
        ).astype(jnp.bfloat16)

        @pl.when(lax.rem(k, HALF) != 0)
        def _():
            total[k] = both
            back(k).start()

        @pl.when(lax.rem(k, HALF) == 0)
        def _():
            ret[k] = both

    def near_pair(pair, carry):
        expert(pair, False)
        return carry

    def far_pair(pair, carry):
        expert(pair, True)
        return carry

    block.wait_recv()
    slot_t[1] = ext[1, :, width + EXTRA :].astype(jnp.float32).T
    lax.fori_loop(HALF + 1, CHIPS, dispatch, 0)
    recv[HALF, core] = pick_rows(HALF)
    share(HALF).start()
    for load in loads:
        load.wait()
    lax.fori_loop(0, 2, near_pair, 0)
    lax.fori_loop(2, 4, far_pair, 0)

    def arrive(k, carry):
        back(k).wait_recv()
        return carry

    def send_back(k, carry):
        finish(k)
        return carry

    half_width = width // 2
    span = half_width // 5

    def spread_of(lo):
        return sel[lo : lo + HALF].reshape(HALF * cap, tok_dev).T.astype(jnp.bfloat16)

    lax.fori_loop(HALF + 1, CHIPS, arrive, 0)
    spread_far = spread_of(HALF)
    for h in range(2):
        def add_far(t, c):
            cols = pl.ds(pl.multiple_of(h * half_width + t * span, span), span)
            got = ret[HALF:, :, cols].reshape(HALF * cap, span)
            into = pl.ds(pl.multiple_of(t * span, span), span)
            partial[h, :, into] = jnp.dot(
                spread_far, got, preferred_element_type=jnp.float32
            ).astype(jnp.bfloat16)
            return c

        lax.fori_loop(0, 5, add_far, 0)
        sum_piece(h).start()

    lax.fori_loop(0, HALF, send_back, 0)
    lax.fori_loop(1, HALF, arrive, 0)
    spread_near = spread_of(0)
    for h in range(2):
        sum_piece(h).wait_recv()

        def gather(t, c):
            cols = pl.ds(pl.multiple_of(h * half_width + t * span, span), span)
            got = ret[:HALF, :, cols].reshape(HALF * cap, span)
            from_far = landed[h, :, pl.ds(pl.multiple_of(t * span, span), span)]
            out_ref[:, cols] = (
                jnp.dot(spread_near, got, preferred_element_type=jnp.float32)
                + from_far.astype(jnp.float32)
            ).astype(out_ref.dtype)
            return c

        lax.fori_loop(0, 5, gather, 0)

    block.wait_send()
    for h in range(2):
        sum_piece(h).wait_send()

    def drain(k, carry):
        first(k).wait_send()
        back(k).wait_send()
        return carry

    lax.fori_loop(1, HALF, drain, 0)
    lax.fori_loop(HALF + 1, CHIPS, drain, 0)

    def drain_sibling(k, carry):
        share(k).wait_send()
        cross(k).wait_send()
        return carry

    lax.fori_loop(0, CHIPS, drain_sibling, 0)


def paired_body(tokens, routes, gate_quanta, gate_weight, up_weight, down_weight):
    tok_dev, width = tokens.shape
    experts = lax.axis_size("group")
    cap = 4 * tok_dev * routes.shape[1] // (3 * experts)
    hid = gate_weight.shape[2]
    bf, f32 = jnp.bfloat16, jnp.float32
    dma = pltpu.SemaphoreType.DMA
    vmem = pl.BlockSpec(memory_space=pltpu.VMEM)
    hbm = pl.BlockSpec(memory_space=pl.ANY)
    return pl.pallas_call(
        paired_kernel,
        out_shape=jax.ShapeDtypeStruct((tok_dev, width), bf),
        in_specs=[vmem, vmem, vmem, hbm, hbm, hbm],
        out_specs=vmem,
        scratch_shapes=[
            pltpu.VMEM((width, hid), bf),
            pltpu.VMEM((width, hid), bf),
            pltpu.VMEM((hid, width), bf),
            pltpu.VMEM((2, tok_dev, width + 2 * EXTRA), bf),
            pltpu.VMEM((2, 128, tok_dev), f32),
            pltpu.VMEM((CHIPS, cap, tok_dev), f32),
            pltpu.VMEM((CHIPS, cap, width + EXTRA), bf),
            pltpu.VMEM((CHIPS, 2, cap, width + EXTRA), bf),
            pltpu.VMEM((4 * cap, hid), bf),
            pltpu.VMEM((4 * cap, 128), f32),
            pltpu.VMEM((CHIPS, 2, cap, width), bf),
            pltpu.VMEM((CHIPS, cap, width), bf),
            pltpu.VMEM((CHIPS, cap, width), bf),
            pltpu.VMEM((CHIPS, cap, width), bf),
            pltpu.VMEM((2, tok_dev, width // 2), bf),
            pltpu.VMEM((2, tok_dev, width // 2), bf),
            dma((3,)),
            dma((1,)), dma((1,)), dma((2,)), dma((2,)),
        ] + [dma((CHIPS,))] * 8,
        compiler_params=pltpu.CompilerParams(
            collective_id=0, has_side_effects=True, vmem_limit_bytes=52 * 1024 * 1024
        ),
        cost_estimate=pl.CostEstimate(
            flops=6 * 16 * cap * width * hid, bytes_accessed=6 * width * hid, transcendentals=0
        ),
    )(tokens, routes, gate_quanta, gate_weight, up_weight, down_weight)


def expert_apply(received, gate_weight, up_weight, down_weight):
    senders = received.shape[0]
    slots_here = received.shape[1]
    inputs = received.reshape(senders * slots_here, received.shape[2])
    gate_part = jnp.dot(inputs, gate_weight[0], preferred_element_type=jnp.float32)
    up_part = jnp.dot(inputs, up_weight[0], preferred_element_type=jnp.float32)
    activ = (jax.nn.silu(gate_part) * up_part).astype(jnp.bfloat16)
    produced = jnp.dot(activ, down_weight[0], preferred_element_type=jnp.float32).astype(
        jnp.bfloat16
    )
    return produced.reshape(senders, slots_here, produced.shape[1])


def body(tokens, routes, gate_quanta, gate_weight, up_weight, down_weight):
    experts = lax.axis_size("group")
    tok_dev = tokens.shape[0]
    width = tokens.shape[1]
    topk = routes.shape[1]
    capacity = 4 * tok_dev * topk // (3 * experts)
    expert_ids = jnp.arange(experts, dtype=jnp.int32)
    matches = routes[:, :, None] == expert_ids[None, None, :]
    picked = jnp.sum(matches.astype(jnp.int32), axis=1)
    weight_quanta = jnp.sum(jnp.where(matches, gate_quanta[:, :, None], 0), axis=1)
    ranking = jnp.cumsum(picked, axis=0) - picked
    slot_of = jnp.where((picked == 1) & (ranking < capacity), ranking, -1)
    contract = (((0,), (0,)), ((), ()))
    selector = slot_of.T[:, None, :] == jnp.arange(capacity, dtype=jnp.int32)[None, :, None]
    selector_float = selector.astype(jnp.float32)
    selector_bf = selector.astype(jnp.bfloat16).reshape(experts * capacity, tok_dev)
    outgoing = jnp.dot(selector_bf, tokens, preferred_element_type=jnp.float32).astype(jnp.bfloat16)
    outgoing = outgoing.reshape(experts, capacity, width)
    produced = expert_apply(
        lax.all_to_all(outgoing, "group", split_axis=0, concat_axis=0, tiled=True),
        gate_weight,
        up_weight,
        down_weight,
    )
    returned = lax.all_to_all(produced, "group", split_axis=0, concat_axis=0, tiled=True)
    upper_part = (weight_quanta // 256).astype(jnp.float32).T / 256.0
    lower_part = (weight_quanta % 256).astype(jnp.float32).T / 65536.0
    combine_upper = (
        (selector_float * upper_part[:, None, :])
        .astype(jnp.bfloat16)
        .reshape(experts * capacity, tok_dev)
    )
    combine_lower = (
        (selector_float * lower_part[:, None, :])
        .astype(jnp.bfloat16)
        .reshape(experts * capacity, tok_dev)
    )
    flat_rows = returned.reshape(experts * capacity, width)
    running = lax.dot_general(
        combine_upper, flat_rows, contract, preferred_element_type=jnp.float32
    )
    running = running + lax.dot_general(
        combine_lower, flat_rows, contract, preferred_element_type=jnp.float32
    )
    return running.astype(jnp.bfloat16)


def solution(mesh):
    placed = (
        P(("parts", "group"), None),
        P(("parts", "group"), None),
        P(("parts", "group"), None),
        P("group", None, None),
        P("group", None, None),
        P("group", None, None),
    )
    chosen = paired_body if mesh.shape["group"] == 2 * CHIPS else body
    return jax.shard_map(
        chosen, mesh=mesh, in_specs=placed, out_specs=P(("parts", "group"), None), check_vma=False
    )
```

```python
import jax
import jax.numpy as jnp
from jax import lax
from jax.experimental import pallas as pl
from jax.experimental.pallas import tpu as pltpu
from jax.sharding import PartitionSpec as P

MESH = pl.DeviceIdType.MESH
CHIPS = 8
HALF = CHIPS // 2
EXTRA = 128


def flip(chip, k):
    low = lax.rem(chip + k, 2)
    mid = lax.rem(chip // 2 + k // 2, 2)
    high = lax.rem(chip // 4 + k // 4, 2)
    return high * 4 + mid * 2 + low


def paired_kernel(
    tok_ref, routes_ref, quanta_ref, gw_hbm, uw_hbm, dw_hbm, out_ref,
    gw, uw, dw, ext, slot_t, sel, outgoing, recv, activ, weight, contrib, sib, total, ret,
    partial, landed, w_sem, block_send, block_recv, part_send, part_recv, send1, recv1, send2, recv2, send3, recv3, send4, recv4,
):
    part = lax.axis_index("parts")
    me = lax.axis_index("group")
    chip, core = me // 2, lax.rem(me, 2)
    other = 1 - core
    sibling = (part, chip * 2 + other)
    tok_dev, width = tok_ref.shape
    cap = sel.shape[1]
    hid = gw.shape[1]

    loads = [
        pltpu.make_async_copy(gw_hbm.at[0], gw, w_sem.at[0]),
        pltpu.make_async_copy(uw_hbm.at[0], uw, w_sem.at[1]),
        pltpu.make_async_copy(dw_hbm.at[0], dw, w_sem.at[2]),
    ]
    for load in loads:
        load.start()

    barrier = pltpu.get_barrier_semaphore()
    for k in range(1, HALF + 1):
        pl.semaphore_signal(
            barrier, inc=1, device_id=(part, flip(chip, k) * 2 + core), device_id_type=MESH
        )
    pl.semaphore_signal(barrier, inc=1, device_id=sibling, device_id_type=MESH)

    lanes = lax.broadcasted_iota(jnp.int32, (tok_dev, 128), 1)
    picked = jnp.zeros((tok_dev, 128), jnp.float32)
    quanta = jnp.zeros((tok_dev, 128), jnp.int32)
    for k in range(routes_ref.shape[1]):
        route = routes_ref[:, k : k + 1]
        picked += (route == lanes).astype(jnp.float32)
        quanta += jnp.where(
            (route == lanes) | (route == lanes - 16), quanta_ref[:, k : k + 1], 0
        )
    upper = (quanta // 256).astype(jnp.float32) / 256.0
    lower = (quanta % 256).astype(jnp.float32) / 65536.0
    before = (lax.broadcasted_iota(jnp.int32, (tok_dev, tok_dev), 1)
              < lax.broadcasted_iota(jnp.int32, (tok_dev, tok_dev), 0))
    ranking = jnp.dot(
        before.astype(jnp.bfloat16), picked.astype(jnp.bfloat16),
        preferred_element_type=jnp.float32,
    )
    slots = jnp.where(picked > 0.5, ranking, -1.0)
    slot_t[0] = slots.T
    ext[0, :, :width] = tok_ref[...]
    marks = jnp.where(lanes < 16, upper, lower)
    ext[0, :, width : width + EXTRA] = marks.astype(jnp.bfloat16)
    ext[0, :, width + EXTRA :] = slots.astype(jnp.bfloat16)
    slot_ids = lax.broadcasted_iota(jnp.int32, (cap, tok_dev), 0).astype(jnp.float32)

    pl.semaphore_wait(barrier, HALF + 1)

    mirror = (part, flip(chip, HALF) * 2 + core)
    block = pltpu.make_async_remote_copy(
        src_ref=ext.at[0], dst_ref=ext.at[1],
        send_sem=block_send.at[0], recv_sem=block_recv.at[0],
        device_id=mirror, device_id_type=MESH)
    block.start()

    def first(k):
        return pltpu.make_async_remote_copy(
            src_ref=outgoing.at[k], dst_ref=recv.at[k, core],
            send_sem=send1.at[k], recv_sem=recv1.at[k],
            device_id=(part, flip(chip, lax.rem(k, HALF)) * 2 + core), device_id_type=MESH)

    def share_from(src, k):
        return pltpu.make_async_remote_copy(
            src_ref=src, dst_ref=recv.at[k, core],
            send_sem=send2.at[k], recv_sem=recv2.at[k],
            device_id=sibling, device_id_type=MESH)

    def share(k):
        return share_from(recv.at[k, core], k)

    def share_in(k):
        return pltpu.make_async_remote_copy(
            src_ref=recv.at[k, other], dst_ref=recv.at[k, other],
            send_sem=send2.at[k], recv_sem=recv2.at[k],
            device_id=sibling, device_id_type=MESH)

    def cross(k):
        return pltpu.make_async_remote_copy(
            src_ref=contrib.at[k, other], dst_ref=sib.at[k],
            send_sem=send3.at[k], recv_sem=recv3.at[k],
            device_id=sibling, device_id_type=MESH)

    def back(h, k):
        cols = pl.ds(h * (width // 2), width // 2)
        return pltpu.make_async_remote_copy(
            src_ref=total.at[k, :, cols], dst_ref=ret.at[k, :, cols],
            send_sem=send4.at[h, k], recv_sem=recv4.at[h, k],
            device_id=(part, flip(chip, lax.rem(k, HALF)) * 2 + core), device_id_type=MESH)

    def sum_piece(h):
        return pltpu.make_async_remote_copy(
            src_ref=partial.at[h], dst_ref=landed.at[h],
            send_sem=part_send.at[h], recv_sem=part_recv.at[h],
            device_id=mirror, device_id_type=MESH)

    def pick_rows(k):
        dest = flip(chip, lax.rem(k, HALF))
        held = k // HALF
        chosen = (slot_t[held, pl.ds(2 * dest, 1), :] == slot_ids).astype(jnp.float32)
        sel[k] = chosen
        return jnp.dot(
            chosen.astype(jnp.bfloat16), ext[held, :, : width + EXTRA],
            preferred_element_type=jnp.float32,
        ).astype(jnp.bfloat16)

    def dispatch(k, carry):
        outgoing[k] = pick_rows(k)
        first(k).start()
        return carry

    lax.fori_loop(1, HALF, dispatch, 0)
    recv[0, core] = pick_rows(0)
    share(0).start()
    rows = 4 * cap
    lane_ids = lax.broadcasted_iota(jnp.int32, (rows, EXTRA), 1)

    def expert(pair, far):
        base = 2 * pair
        local = 4 if far else 0

        def forward(k):
            first(k).wait_recv()
            share(k).start()

        forward(base + 1)

        @pl.when(base != local)
        def _():
            forward(base)

        share_in(base + 1).wait_recv()
        share_in(base).wait_recv()

        def hidden(t, c):
            cols = pl.ds(pl.multiple_of(t * 256, 256), 256)
            x = recv[pl.ds(base, 2), :, :, :width].reshape(rows, width)
            g = jnp.dot(x, gw[:, cols], preferred_element_type=jnp.float32)
            u = jnp.dot(x, uw[:, cols], preferred_element_type=jnp.float32)
            activ[:, cols] = (g / (1.0 + jnp.exp(-g)) * u).astype(jnp.bfloat16)
            return c

        lax.fori_loop(0, hid // 256, hidden, 0)
        marks = recv[pl.ds(base, 2), :, :, width:].reshape(rows, EXTRA).astype(jnp.float32)
        mine = (lane_ids == me) | (lane_ids == me + 16)
        weight[...] = jnp.broadcast_to(
            jnp.sum(jnp.where(mine, marks, 0.0), axis=1, keepdims=True), (rows, 128))

        def down(t, c):
            cols = pl.ds(pl.multiple_of(t * 512, 512), 512)
            o = jnp.dot(activ[...], dw[:, cols], preferred_element_type=jnp.float32)
            o = o * weight[:, :1]
            contrib[pl.ds(base, 2), :, :, cols] = o.astype(jnp.bfloat16).reshape(2, 2, cap, 512)
            return c

        lax.fori_loop(0, width // 512, down, 0)
        cross(base + 1).start()
        cross(base).start()
        if far:
            finish_pair(base)

    def finish_pair(base):
        finish(base + 1)
        finish(base)
        for h in range(2):
            back(h, base + 1).start()

            @pl.when(lax.rem(base, HALF) != 0)
            def _():
                back(h, base).start()

    def finish(k):
        cross(k).wait_recv()
        both = (
            contrib[k, core].astype(jnp.float32) + sib[k].astype(jnp.float32)
        ).astype(jnp.bfloat16)

        @pl.when(lax.rem(k, HALF) != 0)
        def _():
            total[k] = both

        @pl.when(lax.rem(k, HALF) == 0)
        def _():
            ret[k] = both

    def near_pair(pair, carry):
        expert(pair, False)
        return carry

    def far_pair(pair, carry):
        expert(pair, True)
        return carry

    block.wait_recv()
    slot_t[1] = ext[1, :, width + EXTRA :].astype(jnp.float32).T
    lax.fori_loop(HALF + 1, CHIPS, dispatch, 0)
    recv[HALF, core] = pick_rows(HALF)
    share(HALF).start()
    for load in loads:
        load.wait()
    lax.fori_loop(0, 2, near_pair, 0)
    for pair in range(2):
        finish_pair(2 * pair)
    lax.fori_loop(2, 4, far_pair, 0)

    def arrive(h):
        def one(k, carry):
            back(h, k).wait_recv()
            return carry

        return one

    half_width = width // 2
    span = half_width // 5

    def spread_of(lo):
        return sel[lo : lo + HALF].reshape(HALF * cap, tok_dev).T.astype(jnp.bfloat16)

    spread_far = spread_of(HALF)
    for h in range(2):
        lax.fori_loop(HALF + 1, CHIPS, arrive(h), 0)

        def add_far(t, c):
            cols = pl.ds(pl.multiple_of(h * half_width + t * span, span), span)
            got = ret[HALF:, :, cols].reshape(HALF * cap, span)
            into = pl.ds(pl.multiple_of(t * span, span), span)
            partial[h, :, into] = jnp.dot(
                spread_far, got, preferred_element_type=jnp.float32
            ).astype(jnp.bfloat16)
            return c

        lax.fori_loop(0, 5, add_far, 0)
        sum_piece(h).start()

    for h in range(2):
        lax.fori_loop(1, HALF, arrive(h), 0)
    spread_near = spread_of(0)
    for h in range(2):
        sum_piece(h).wait_recv()

        def gather(t, c):
            cols = pl.ds(pl.multiple_of(h * half_width + t * span, span), span)
            got = ret[:HALF, :, cols].reshape(HALF * cap, span)
            from_far = landed[h, :, pl.ds(pl.multiple_of(t * span, span), span)]
            out_ref[:, cols] = (
                jnp.dot(spread_near, got, preferred_element_type=jnp.float32)
                + from_far.astype(jnp.float32)
            ).astype(out_ref.dtype)
            return c

        lax.fori_loop(0, 5, gather, 0)

    block.wait_send()
    for h in range(2):
        sum_piece(h).wait_send()

    def drain(k, carry):
        first(k).wait_send()
        back(0, k).wait_send()
        back(1, k).wait_send()
        return carry

    lax.fori_loop(1, HALF, drain, 0)
    lax.fori_loop(HALF + 1, CHIPS, drain, 0)

    def drain_sibling(k, carry):
        share(k).wait_send()
        cross(k).wait_send()
        return carry

    lax.fori_loop(0, CHIPS, drain_sibling, 0)


def paired_body(tokens, routes, gate_quanta, gate_weight, up_weight, down_weight):
    tok_dev, width = tokens.shape
    experts = lax.axis_size("group")
    cap = 4 * tok_dev * routes.shape[1] // (3 * experts)
    hid = gate_weight.shape[2]
    bf, f32 = jnp.bfloat16, jnp.float32
    dma = pltpu.SemaphoreType.DMA
    vmem = pl.BlockSpec(memory_space=pltpu.VMEM)
    hbm = pl.BlockSpec(memory_space=pl.ANY)
    return pl.pallas_call(
        paired_kernel,
        out_shape=jax.ShapeDtypeStruct((tok_dev, width), bf),
        in_specs=[vmem, vmem, vmem, hbm, hbm, hbm],
        out_specs=vmem,
        scratch_shapes=[
            pltpu.VMEM((width, hid), bf),
            pltpu.VMEM((width, hid), bf),
            pltpu.VMEM((hid, width), bf),
            pltpu.VMEM((2, tok_dev, width + 2 * EXTRA), bf),
            pltpu.VMEM((2, 128, tok_dev), f32),
            pltpu.VMEM((CHIPS, cap, tok_dev), f32),
            pltpu.VMEM((CHIPS, cap, width + EXTRA), bf),
            pltpu.VMEM((CHIPS, 2, cap, width + EXTRA), bf),
            pltpu.VMEM((4 * cap, hid), bf),
            pltpu.VMEM((4 * cap, 128), f32),
            pltpu.VMEM((CHIPS, 2, cap, width), bf),
            pltpu.VMEM((CHIPS, cap, width), bf),
            pltpu.VMEM((CHIPS, cap, width), bf),
            pltpu.VMEM((CHIPS, cap, width), bf),
            pltpu.VMEM((2, tok_dev, width // 2), bf),
            pltpu.VMEM((2, tok_dev, width // 2), bf),
            dma((3,)),
            dma((1,)), dma((1,)), dma((2,)), dma((2,)),
        ] + [dma((CHIPS,))] * 6 + [dma((2, CHIPS))] * 2,
        compiler_params=pltpu.CompilerParams(
            collective_id=0, has_side_effects=True, vmem_limit_bytes=52 * 1024 * 1024
        ),
        cost_estimate=pl.CostEstimate(
            flops=6 * 16 * cap * width * hid, bytes_accessed=6 * width * hid, transcendentals=0
        ),
    )(tokens, routes, gate_quanta, gate_weight, up_weight, down_weight)


def expert_apply(received, gate_weight, up_weight, down_weight):
    senders = received.shape[0]
    slots_here = received.shape[1]
    inputs = received.reshape(senders * slots_here, received.shape[2])
    gate_part = jnp.dot(inputs, gate_weight[0], preferred_element_type=jnp.float32)
    up_part = jnp.dot(inputs, up_weight[0], preferred_element_type=jnp.float32)
    activ = (jax.nn.silu(gate_part) * up_part).astype(jnp.bfloat16)
    produced = jnp.dot(activ, down_weight[0], preferred_element_type=jnp.float32).astype(
        jnp.bfloat16
    )
    return produced.reshape(senders, slots_here, produced.shape[1])


def body(tokens, routes, gate_quanta, gate_weight, up_weight, down_weight):
    experts = lax.axis_size("group")
    tok_dev = tokens.shape[0]
    width = tokens.shape[1]
    topk = routes.shape[1]
    capacity = 4 * tok_dev * topk // (3 * experts)
    expert_ids = jnp.arange(experts, dtype=jnp.int32)
    matches = routes[:, :, None] == expert_ids[None, None, :]
    picked = jnp.sum(matches.astype(jnp.int32), axis=1)
    weight_quanta = jnp.sum(jnp.where(matches, gate_quanta[:, :, None], 0), axis=1)
    ranking = jnp.cumsum(picked, axis=0) - picked
    slot_of = jnp.where((picked == 1) & (ranking < capacity), ranking, -1)
    contract = (((0,), (0,)), ((), ()))
    selector = slot_of.T[:, None, :] == jnp.arange(capacity, dtype=jnp.int32)[None, :, None]
    selector_float = selector.astype(jnp.float32)
    selector_bf = selector.astype(jnp.bfloat16).reshape(experts * capacity, tok_dev)
    outgoing = jnp.dot(selector_bf, tokens, preferred_element_type=jnp.float32).astype(jnp.bfloat16)
    outgoing = outgoing.reshape(experts, capacity, width)
    produced = expert_apply(
        lax.all_to_all(outgoing, "group", split_axis=0, concat_axis=0, tiled=True),
        gate_weight,
        up_weight,
        down_weight,
    )
    returned = lax.all_to_all(produced, "group", split_axis=0, concat_axis=0, tiled=True)
    upper_part = (weight_quanta // 256).astype(jnp.float32).T / 256.0
    lower_part = (weight_quanta % 256).astype(jnp.float32).T / 65536.0
    combine_upper = (
        (selector_float * upper_part[:, None, :])
        .astype(jnp.bfloat16)
        .reshape(experts * capacity, tok_dev)
    )
    combine_lower = (
        (selector_float * lower_part[:, None, :])
        .astype(jnp.bfloat16)
        .reshape(experts * capacity, tok_dev)
    )
    flat_rows = returned.reshape(experts * capacity, width)
    running = lax.dot_general(
        combine_upper, flat_rows, contract, preferred_element_type=jnp.float32
    )
    running = running + lax.dot_general(
        combine_lower, flat_rows, contract, preferred_element_type=jnp.float32
    )
    return running.astype(jnp.bfloat16)


def solution(mesh):
    placed = (
        P(("parts", "group"), None),
        P(("parts", "group"), None),
        P(("parts", "group"), None),
        P("group", None, None),
        P("group", None, None),
        P("group", None, None),
    )
    chosen = paired_body if mesh.shape["group"] == 2 * CHIPS else body
    return jax.shard_map(
        chosen, mesh=mesh, in_specs=placed, out_specs=P(("parts", "group"), None), check_vma=False
    )
```

```python
import jax
import jax.numpy as jnp
from jax import lax
from jax.experimental import pallas as pl
from jax.experimental.pallas import tpu as pltpu
from jax.sharding import PartitionSpec as P

MESH = pl.DeviceIdType.MESH
CHIPS = 8
HALF = CHIPS // 2
EXTRA = 128


def flip(chip, k):
    low = lax.rem(chip + k, 2)
    mid = lax.rem(chip // 2 + k // 2, 2)
    high = lax.rem(chip // 4 + k // 4, 2)
    return high * 4 + mid * 2 + low


def paired_kernel(
    tok_ref, routes_ref, quanta_ref, gw_hbm, uw_hbm, dw_hbm, out_ref,
    gw, uw, dw, ext, slot_t, sel, outgoing, recv, activ, weight, contrib, sib, total, ret,
    partial, landed, w_sem, block_send, block_recv, part_send, part_recv, send1, recv1, send2, recv2, send3, recv3, send4, recv4,
):
    part = lax.axis_index("parts")
    me = lax.axis_index("group")
    chip, core = me // 2, lax.rem(me, 2)
    other = 1 - core
    sibling = (part, chip * 2 + other)
    tok_dev, width = tok_ref.shape
    cap = sel.shape[1]
    hid = gw.shape[1]

    loads = [
        pltpu.make_async_copy(gw_hbm.at[0], gw, w_sem.at[0]),
        pltpu.make_async_copy(uw_hbm.at[0], uw, w_sem.at[1]),
        pltpu.make_async_copy(dw_hbm.at[0], dw, w_sem.at[2]),
    ]
    for load in loads:
        load.start()

    barrier = pltpu.get_barrier_semaphore()
    for k in range(1, HALF + 1):
        pl.semaphore_signal(
            barrier, inc=1, device_id=(part, flip(chip, k) * 2 + core), device_id_type=MESH
        )
    pl.semaphore_signal(barrier, inc=1, device_id=sibling, device_id_type=MESH)

    subs = lax.broadcasted_iota(jnp.int32, (EXTRA, tok_dev), 0)
    picked = jnp.zeros((EXTRA, tok_dev), jnp.float32)
    quanta = jnp.zeros((EXTRA, tok_dev), jnp.int32)
    for k in range(routes_ref.shape[0]):
        route = routes_ref[k : k + 1, :]
        picked += (route == subs - 32).astype(jnp.float32)
        quanta += jnp.where(
            (route == subs) | (route == subs - 16), quanta_ref[k : k + 1, :], 0
        )
    upper = (quanta // 256).astype(jnp.float32) / 256.0
    lower = (quanta % 256).astype(jnp.float32) / 65536.0
    before = (lax.broadcasted_iota(jnp.int32, (tok_dev, tok_dev), 0)
              < lax.broadcasted_iota(jnp.int32, (tok_dev, tok_dev), 1))
    ranking = jnp.dot(
        picked.astype(jnp.bfloat16), before.astype(jnp.bfloat16),
        preferred_element_type=jnp.float32,
    )
    slots = jnp.where(picked > 0.5, ranking, -1.0)
    marks = jnp.where(subs < 16, upper, jnp.where(subs < 32, lower, slots))
    slot_t[0] = marks
    ext[0, :, :width] = tok_ref[...]
    ext[0, :, width:] = marks.T.astype(jnp.bfloat16)
    slot_ids = lax.broadcasted_iota(jnp.int32, (cap, tok_dev), 0).astype(jnp.float32)

    pl.semaphore_wait(barrier, HALF + 1)

    mirror = (part, flip(chip, HALF) * 2 + core)
    block = pltpu.make_async_remote_copy(
        src_ref=ext.at[0], dst_ref=ext.at[1],
        send_sem=block_send.at[0], recv_sem=block_recv.at[0],
        device_id=mirror, device_id_type=MESH)
    block.start()

    def first(k):
        return pltpu.make_async_remote_copy(
            src_ref=outgoing.at[k], dst_ref=recv.at[k, core],
            send_sem=send1.at[k], recv_sem=recv1.at[k],
            device_id=(part, flip(chip, lax.rem(k, HALF)) * 2 + core), device_id_type=MESH)

    def share_from(src, k):
        return pltpu.make_async_remote_copy(
            src_ref=src, dst_ref=recv.at[k, core],
            send_sem=send2.at[k], recv_sem=recv2.at[k],
            device_id=sibling, device_id_type=MESH)

    def share(k):
        return share_from(recv.at[k, core], k)

    def share_in(k):
        return pltpu.make_async_remote_copy(
            src_ref=recv.at[k, other], dst_ref=recv.at[k, other],
            send_sem=send2.at[k], recv_sem=recv2.at[k],
            device_id=sibling, device_id_type=MESH)

    def cross(k):
        return pltpu.make_async_remote_copy(
            src_ref=contrib.at[k, other], dst_ref=sib.at[k],
            send_sem=send3.at[k], recv_sem=recv3.at[k],
            device_id=sibling, device_id_type=MESH)

    def back(h, k):
        cols = pl.ds(h * (width // 2), width // 2)
        return pltpu.make_async_remote_copy(
            src_ref=total.at[k, :, cols], dst_ref=ret.at[k, :, cols],
            send_sem=send4.at[h, k], recv_sem=recv4.at[h, k],
            device_id=(part, flip(chip, lax.rem(k, HALF)) * 2 + core), device_id_type=MESH)

    def sum_piece(h):
        return pltpu.make_async_remote_copy(
            src_ref=partial.at[h], dst_ref=landed.at[h],
            send_sem=part_send.at[h], recv_sem=part_recv.at[h],
            device_id=mirror, device_id_type=MESH)

    def pick_rows(k):
        dest = flip(chip, lax.rem(k, HALF))
        held = k // HALF
        chosen = (slot_t[held, pl.ds(32 + 2 * dest, 1), :] == slot_ids).astype(jnp.float32)
        sel[k] = chosen
        return jnp.dot(
            chosen.astype(jnp.bfloat16), ext[held],
            preferred_element_type=jnp.float32,
        ).astype(jnp.bfloat16)

    def dispatch(k, carry):
        outgoing[k] = pick_rows(k)
        first(k).start()
        return carry

    lax.fori_loop(1, HALF, dispatch, 0)
    recv[0, core] = pick_rows(0)
    share(0).start()
    rows = 4 * cap
    lane_ids = lax.broadcasted_iota(jnp.int32, (rows, EXTRA), 1)

    def expert(pair, far):
        base = 2 * pair
        local = 4 if far else 0

        def forward(k):
            first(k).wait_recv()
            share(k).start()

        forward(base + 1)

        @pl.when(base != local)
        def _():
            forward(base)

        share_in(base + 1).wait_recv()
        share_in(base).wait_recv()

        def hidden(t, c):
            cols = pl.ds(pl.multiple_of(t * 256, 256), 256)
            x = recv[pl.ds(base, 2), :, :, :width].reshape(rows, width)
            g = jnp.dot(x, gw[:, cols], preferred_element_type=jnp.float32)
            u = jnp.dot(x, uw[:, cols], preferred_element_type=jnp.float32)
            activ[:, cols] = (g / (1.0 + jnp.exp(-g)) * u).astype(jnp.bfloat16)
            return c

        lax.fori_loop(0, hid // 256, hidden, 0)
        marks = recv[pl.ds(base, 2), :, :, width:].reshape(rows, EXTRA).astype(jnp.float32)
        mine = (lane_ids == me) | (lane_ids == me + 16)
        weight[...] = jnp.broadcast_to(
            jnp.sum(jnp.where(mine, marks, 0.0), axis=1, keepdims=True), (rows, 128))

        def down(t, c):
            cols = pl.ds(pl.multiple_of(t * 512, 512), 512)
            o = jnp.dot(activ[...], dw[:, cols], preferred_element_type=jnp.float32)
            o = o * weight[:, :1]
            contrib[pl.ds(base, 2), :, :, cols] = o.astype(jnp.bfloat16).reshape(2, 2, cap, 512)
            return c

        lax.fori_loop(0, width // 512, down, 0)
        cross(base + 1).start()
        cross(base).start()
        if far:
            finish_pair(base)

    def finish_pair(base):
        finish(base + 1)
        finish(base)
        for h in range(2):
            back(h, base + 1).start()

            @pl.when(lax.rem(base, HALF) != 0)
            def _():
                back(h, base).start()

    def finish(k):
        cross(k).wait_recv()
        both = (
            contrib[k, core].astype(jnp.float32) + sib[k].astype(jnp.float32)
        ).astype(jnp.bfloat16)

        @pl.when(lax.rem(k, HALF) != 0)
        def _():
            total[k] = both

        @pl.when(lax.rem(k, HALF) == 0)
        def _():
            ret[k] = both

    def near_pair(pair, carry):
        expert(pair, False)
        return carry

    def far_pair(pair, carry):
        expert(pair, True)
        return carry

    block.wait_recv()
    slot_t[1] = ext[1, :, width:].astype(jnp.float32).T
    lax.fori_loop(HALF + 1, CHIPS, dispatch, 0)
    recv[HALF, core] = pick_rows(HALF)
    share(HALF).start()
    for load in loads:
        load.wait()
    lax.fori_loop(0, 2, near_pair, 0)
    for pair in range(2):
        finish_pair(2 * pair)
    lax.fori_loop(2, 4, far_pair, 0)

    def arrive(h):
        def one(k, carry):
            back(h, k).wait_recv()
            return carry

        return one

    half_width = width // 2
    span = half_width // 5

    def spread_of(lo):
        return sel[lo : lo + HALF].reshape(HALF * cap, tok_dev).T.astype(jnp.bfloat16)

    spread_far = spread_of(HALF)
    for h in range(2):
        lax.fori_loop(HALF + 1, CHIPS, arrive(h), 0)

        def add_far(t, c):
            cols = pl.ds(pl.multiple_of(h * half_width + t * span, span), span)
            got = ret[HALF:, :, cols].reshape(HALF * cap, span)
            into = pl.ds(pl.multiple_of(t * span, span), span)
            partial[h, :, into] = jnp.dot(
                spread_far, got, preferred_element_type=jnp.float32
            ).astype(jnp.bfloat16)
            return c

        lax.fori_loop(0, 5, add_far, 0)
        sum_piece(h).start()

    for h in range(2):
        lax.fori_loop(1, HALF, arrive(h), 0)
    spread_near = spread_of(0)
    for h in range(2):
        sum_piece(h).wait_recv()

        def gather(t, c):
            cols = pl.ds(pl.multiple_of(h * half_width + t * span, span), span)
            got = ret[:HALF, :, cols].reshape(HALF * cap, span)
            from_far = landed[h, :, pl.ds(pl.multiple_of(t * span, span), span)]
            out_ref[:, cols] = (
                jnp.dot(spread_near, got, preferred_element_type=jnp.float32)
                + from_far.astype(jnp.float32)
            ).astype(out_ref.dtype)
            return c

        lax.fori_loop(0, 5, gather, 0)

    block.wait_send()
    for h in range(2):
        sum_piece(h).wait_send()

    def drain(k, carry):
        first(k).wait_send()
        back(0, k).wait_send()
        back(1, k).wait_send()
        return carry

    lax.fori_loop(1, HALF, drain, 0)
    lax.fori_loop(HALF + 1, CHIPS, drain, 0)

    def drain_sibling(k, carry):
        share(k).wait_send()
        cross(k).wait_send()
        return carry

    lax.fori_loop(0, CHIPS, drain_sibling, 0)


def paired_body(tokens, routes, gate_quanta, gate_weight, up_weight, down_weight):
    tok_dev, width = tokens.shape
    experts = lax.axis_size("group")
    cap = 4 * tok_dev * routes.shape[1] // (3 * experts)
    hid = gate_weight.shape[2]
    bf, f32 = jnp.bfloat16, jnp.float32
    dma = pltpu.SemaphoreType.DMA
    vmem = pl.BlockSpec(memory_space=pltpu.VMEM)
    hbm = pl.BlockSpec(memory_space=pl.ANY)
    return pl.pallas_call(
        paired_kernel,
        out_shape=jax.ShapeDtypeStruct((tok_dev, width), bf),
        in_specs=[vmem, vmem, vmem, hbm, hbm, hbm],
        out_specs=vmem,
        scratch_shapes=[
            pltpu.VMEM((width, hid), bf),
            pltpu.VMEM((width, hid), bf),
            pltpu.VMEM((hid, width), bf),
            pltpu.VMEM((2, tok_dev, width + EXTRA), bf),
            pltpu.VMEM((2, 128, tok_dev), f32),
            pltpu.VMEM((CHIPS, cap, tok_dev), f32),
            pltpu.VMEM((CHIPS, cap, width + EXTRA), bf),
            pltpu.VMEM((CHIPS, 2, cap, width + EXTRA), bf),
            pltpu.VMEM((4 * cap, hid), bf),
            pltpu.VMEM((4 * cap, 128), f32),
            pltpu.VMEM((CHIPS, 2, cap, width), bf),
            pltpu.VMEM((CHIPS, cap, width), bf),
            pltpu.VMEM((CHIPS, cap, width), bf),
            pltpu.VMEM((CHIPS, cap, width), bf),
            pltpu.VMEM((2, tok_dev, width // 2), bf),
            pltpu.VMEM((2, tok_dev, width // 2), bf),
            dma((3,)),
            dma((1,)), dma((1,)), dma((2,)), dma((2,)),
        ] + [dma((CHIPS,))] * 6 + [dma((2, CHIPS))] * 2,
        compiler_params=pltpu.CompilerParams(
            collective_id=0, has_side_effects=True, vmem_limit_bytes=52 * 1024 * 1024
        ),
        cost_estimate=pl.CostEstimate(
            flops=6 * 16 * cap * width * hid, bytes_accessed=6 * width * hid, transcendentals=0
        ),
    )(tokens, routes.T, gate_quanta.T, gate_weight, up_weight, down_weight)


def expert_apply(received, gate_weight, up_weight, down_weight):
    senders = received.shape[0]
    slots_here = received.shape[1]
    inputs = received.reshape(senders * slots_here, received.shape[2])
    gate_part = jnp.dot(inputs, gate_weight[0], preferred_element_type=jnp.float32)
    up_part = jnp.dot(inputs, up_weight[0], preferred_element_type=jnp.float32)
    activ = (jax.nn.silu(gate_part) * up_part).astype(jnp.bfloat16)
    produced = jnp.dot(activ, down_weight[0], preferred_element_type=jnp.float32).astype(
        jnp.bfloat16
    )
    return produced.reshape(senders, slots_here, produced.shape[1])


def body(tokens, routes, gate_quanta, gate_weight, up_weight, down_weight):
    experts = lax.axis_size("group")
    tok_dev = tokens.shape[0]
    width = tokens.shape[1]
    topk = routes.shape[1]
    capacity = 4 * tok_dev * topk // (3 * experts)
    expert_ids = jnp.arange(experts, dtype=jnp.int32)
    matches = routes[:, :, None] == expert_ids[None, None, :]
    picked = jnp.sum(matches.astype(jnp.int32), axis=1)
    weight_quanta = jnp.sum(jnp.where(matches, gate_quanta[:, :, None], 0), axis=1)
    ranking = jnp.cumsum(picked, axis=0) - picked
    slot_of = jnp.where((picked == 1) & (ranking < capacity), ranking, -1)
    contract = (((0,), (0,)), ((), ()))
    selector = slot_of.T[:, None, :] == jnp.arange(capacity, dtype=jnp.int32)[None, :, None]
    selector_float = selector.astype(jnp.float32)
    selector_bf = selector.astype(jnp.bfloat16).reshape(experts * capacity, tok_dev)
    outgoing = jnp.dot(selector_bf, tokens, preferred_element_type=jnp.float32).astype(jnp.bfloat16)
    outgoing = outgoing.reshape(experts, capacity, width)
    produced = expert_apply(
        lax.all_to_all(outgoing, "group", split_axis=0, concat_axis=0, tiled=True),
        gate_weight,
        up_weight,
        down_weight,
    )
    returned = lax.all_to_all(produced, "group", split_axis=0, concat_axis=0, tiled=True)
    upper_part = (weight_quanta // 256).astype(jnp.float32).T / 256.0
    lower_part = (weight_quanta % 256).astype(jnp.float32).T / 65536.0
    combine_upper = (
        (selector_float * upper_part[:, None, :])
        .astype(jnp.bfloat16)
        .reshape(experts * capacity, tok_dev)
    )
    combine_lower = (
        (selector_float * lower_part[:, None, :])
        .astype(jnp.bfloat16)
        .reshape(experts * capacity, tok_dev)
    )
    flat_rows = returned.reshape(experts * capacity, width)
    running = lax.dot_general(
        combine_upper, flat_rows, contract, preferred_element_type=jnp.float32
    )
    running = running + lax.dot_general(
        combine_lower, flat_rows, contract, preferred_element_type=jnp.float32
    )
    return running.astype(jnp.bfloat16)


def solution(mesh):
    placed = (
        P(("parts", "group"), None),
        P(("parts", "group"), None),
        P(("parts", "group"), None),
        P("group", None, None),
        P("group", None, None),
        P("group", None, None),
    )
    chosen = paired_body if mesh.shape["group"] == 2 * CHIPS else body
    return jax.shard_map(
        chosen, mesh=mesh, in_specs=placed, out_specs=P(("parts", "group"), None), check_vma=False
    )
```

```python
import jax
import jax.numpy as jnp
from jax import lax
from jax.experimental import pallas as pl
from jax.experimental.pallas import tpu as pltpu
from jax.sharding import PartitionSpec as P

MESH = pl.DeviceIdType.MESH
CHIPS = 8
HALF = CHIPS // 2
EXTRA = 128


def flip(chip, k):
    low = lax.rem(chip + k, 2)
    mid = lax.rem(chip // 2 + k // 2, 2)
    high = lax.rem(chip // 4 + k // 4, 2)
    return high * 4 + mid * 2 + low


def paired_kernel(
    tok_ref, routes_ref, quanta_ref, gw_hbm, uw_hbm, dw_hbm, out_ref,
    gw, uw, dw, ext, slot_t, sel, outgoing, recv, activ, weight, contrib, sib, total, ret,
    partial, landed, w_sem, block_send, block_recv, part_send, part_recv, send1, recv1, send2, recv2, send3, recv3, send4, recv4,
):
    part = lax.axis_index("parts")
    me = lax.axis_index("group")
    chip, core = me // 2, lax.rem(me, 2)
    other = 1 - core
    sibling = (part, chip * 2 + other)
    tok_dev, width = tok_ref.shape
    cap = sel.shape[1]
    hid = gw.shape[1]

    loads = [
        pltpu.make_async_copy(gw_hbm.at[0], gw, w_sem.at[0]),
        pltpu.make_async_copy(uw_hbm.at[0], uw, w_sem.at[1]),
        pltpu.make_async_copy(dw_hbm.at[0], dw, w_sem.at[2]),
    ]
    for load in loads:
        load.start()

    barrier = pltpu.get_barrier_semaphore()
    for k in range(1, HALF + 1):
        pl.semaphore_signal(
            barrier, inc=1, device_id=(part, flip(chip, k) * 2 + core), device_id_type=MESH
        )
    pl.semaphore_signal(barrier, inc=1, device_id=sibling, device_id_type=MESH)

    subs = lax.broadcasted_iota(jnp.int32, (EXTRA, tok_dev), 0)
    picked = jnp.zeros((EXTRA, tok_dev), jnp.float32)
    quanta = jnp.zeros((EXTRA, tok_dev), jnp.int32)
    for k in range(routes_ref.shape[0]):
        route = routes_ref[k : k + 1, :]
        picked += (route == subs - 32).astype(jnp.float32)
        quanta += jnp.where(
            (route == subs) | (route == subs - 16), quanta_ref[k : k + 1, :], 0
        )
    upper = (quanta // 256).astype(jnp.float32) / 256.0
    lower = (quanta % 256).astype(jnp.float32) / 65536.0
    before = (lax.broadcasted_iota(jnp.int32, (tok_dev, tok_dev), 0)
              < lax.broadcasted_iota(jnp.int32, (tok_dev, tok_dev), 1))
    ranking = jnp.dot(
        picked.astype(jnp.bfloat16), before.astype(jnp.bfloat16),
        preferred_element_type=jnp.float32,
    )
    slots = jnp.where(picked > 0.5, ranking, -1.0)
    marks = jnp.where(subs < 16, upper, jnp.where(subs < 32, lower, slots))
    slot_t[0] = marks
    ext[0, :, :width] = tok_ref[...]
    ext[0, :, width:] = marks.T.astype(jnp.bfloat16)
    slot_ids = lax.broadcasted_iota(jnp.int32, (cap, tok_dev), 0).astype(jnp.float32)

    pl.semaphore_wait(barrier, HALF + 1)

    mirror = (part, flip(chip, HALF) * 2 + core)
    block = pltpu.make_async_remote_copy(
        src_ref=ext.at[0], dst_ref=ext.at[1],
        send_sem=block_send.at[0], recv_sem=block_recv.at[0],
        device_id=mirror, device_id_type=MESH)
    block.start()

    def first(k):
        return pltpu.make_async_remote_copy(
            src_ref=outgoing.at[k], dst_ref=recv.at[k, core],
            send_sem=send1.at[k], recv_sem=recv1.at[k],
            device_id=(part, flip(chip, lax.rem(k, HALF)) * 2 + core), device_id_type=MESH)

    def share_from(src, k):
        return pltpu.make_async_remote_copy(
            src_ref=src, dst_ref=recv.at[k, core],
            send_sem=send2.at[k], recv_sem=recv2.at[k],
            device_id=sibling, device_id_type=MESH)

    def share(k):
        return share_from(recv.at[k, core], k)

    def share_in(k):
        return pltpu.make_async_remote_copy(
            src_ref=recv.at[k, other], dst_ref=recv.at[k, other],
            send_sem=send2.at[k], recv_sem=recv2.at[k],
            device_id=sibling, device_id_type=MESH)

    def cross(k):
        return pltpu.make_async_remote_copy(
            src_ref=contrib.at[k, other], dst_ref=sib.at[k],
            send_sem=send3.at[k], recv_sem=recv3.at[k],
            device_id=sibling, device_id_type=MESH)

    def back(h, k):
        cols = pl.ds(h * (width // 2), width // 2)
        return pltpu.make_async_remote_copy(
            src_ref=total.at[k, :, cols], dst_ref=ret.at[k, :, cols],
            send_sem=send4.at[h, k], recv_sem=recv4.at[h, k],
            device_id=(part, flip(chip, lax.rem(k, HALF)) * 2 + core), device_id_type=MESH)

    def sum_piece(h):
        return pltpu.make_async_remote_copy(
            src_ref=partial.at[h], dst_ref=landed.at[h],
            send_sem=part_send.at[h], recv_sem=part_recv.at[h],
            device_id=mirror, device_id_type=MESH)

    def pick_rows(k):
        dest = flip(chip, lax.rem(k, HALF))
        held = k // HALF
        chosen = (slot_t[held, pl.ds(32 + 2 * dest, 1), :] == slot_ids).astype(jnp.float32)
        sel[k] = chosen
        return jnp.dot(
            chosen.astype(jnp.bfloat16), ext[held],
            preferred_element_type=jnp.float32,
        ).astype(jnp.bfloat16)

    def dispatch(k, carry):
        outgoing[k] = pick_rows(k)
        first(k).start()
        return carry

    lax.fori_loop(1, HALF, dispatch, 0)
    recv[0, core] = pick_rows(0)
    share(0).start()
    rows = 4 * cap
    lane_ids = lax.broadcasted_iota(jnp.int32, (rows, EXTRA), 1)

    def expert(pair, far):
        base = 2 * pair
        local = 4 if far else 0

        def forward(k):
            first(k).wait_recv()
            share(k).start()

        forward(base + 1)

        @pl.when(base != local)
        def _():
            forward(base)

        share_in(base + 1).wait_recv()
        share_in(base).wait_recv()

        def hidden(t, c):
            cols = pl.ds(pl.multiple_of(t * 256, 256), 256)
            x = recv[pl.ds(base, 2), :, :, :width].reshape(rows, width)
            g = jnp.dot(x, gw[:, cols], preferred_element_type=jnp.float32)
            u = jnp.dot(x, uw[:, cols], preferred_element_type=jnp.float32)
            activ[:, cols] = (g / (1.0 + jnp.exp(-g)) * u).astype(jnp.bfloat16)
            return c

        lax.fori_loop(0, hid // 256, hidden, 0)
        marks = recv[pl.ds(base, 2), :, :, width:].reshape(rows, EXTRA).astype(jnp.float32)
        mine = (lane_ids == me) | (lane_ids == me + 16)
        weight[...] = jnp.broadcast_to(
            jnp.sum(jnp.where(mine, marks, 0.0), axis=1, keepdims=True), (rows, 128))

        def down(t, c):
            cols = pl.ds(pl.multiple_of(t * 512, 512), 512)
            o = jnp.dot(activ[...], dw[:, cols], preferred_element_type=jnp.float32)
            o = o * weight[:, :1]
            contrib[pl.ds(base, 2), :, :, cols] = o.astype(jnp.bfloat16).reshape(2, 2, cap, 512)
            return c

        lax.fori_loop(0, width // 512, down, 0)
        cross(base + 1).start()
        cross(base).start()
        if far:
            finish_pair(base)

    def finish_pair(base):
        finish(base + 1)
        finish(base)
        for h in range(2):
            back(h, base + 1).start()

            @pl.when(lax.rem(base, HALF) != 0)
            def _():
                back(h, base).start()

    def finish(k):
        cross(k).wait_recv()
        both = (
            contrib[k, core].astype(jnp.float32) + sib[k].astype(jnp.float32)
        ).astype(jnp.bfloat16)

        @pl.when(lax.rem(k, HALF) != 0)
        def _():
            total[k] = both

        @pl.when(lax.rem(k, HALF) == 0)
        def _():
            ret[k] = both

    def near_pair(pair, carry):
        expert(pair, False)
        return carry

    def far_pair(pair, carry):
        expert(pair, True)
        return carry

    block.wait_recv()
    slot_t[1] = ext[1, :, width:].astype(jnp.float32).T
    lax.fori_loop(HALF + 1, CHIPS, lambda k, c: dispatch(CHIPS + HALF - k, c), 0)
    recv[HALF, core] = pick_rows(HALF)
    share(HALF).start()
    for load in loads:
        load.wait()
    lax.fori_loop(0, 2, near_pair, 0)
    for pair in range(2):
        finish_pair(2 * pair)
    lax.fori_loop(2, 4, far_pair, 0)

    def arrive(h):
        def one(k, carry):
            back(h, k).wait_recv()
            return carry

        return one

    half_width = width // 2
    span = half_width // 5

    def spread_of(lo):
        return sel[lo : lo + HALF].reshape(HALF * cap, tok_dev).T.astype(jnp.bfloat16)

    spread_far = spread_of(HALF)
    for h in range(2):
        lax.fori_loop(HALF + 1, CHIPS, arrive(h), 0)

        def add_far(t, c):
            cols = pl.ds(pl.multiple_of(h * half_width + t * span, span), span)
            got = ret[HALF:, :, cols].reshape(HALF * cap, span)
            into = pl.ds(pl.multiple_of(t * span, span), span)
            partial[h, :, into] = jnp.dot(
                spread_far, got, preferred_element_type=jnp.float32
            ).astype(jnp.bfloat16)
            return c

        lax.fori_loop(0, 5, add_far, 0)
        sum_piece(h).start()

    for h in range(2):
        lax.fori_loop(1, HALF, arrive(h), 0)
    spread_near = spread_of(0)
    for h in range(2):
        sum_piece(h).wait_recv()

        def gather(t, c):
            cols = pl.ds(pl.multiple_of(h * half_width + t * span, span), span)
            got = ret[:HALF, :, cols].reshape(HALF * cap, span)
            from_far = landed[h, :, pl.ds(pl.multiple_of(t * span, span), span)]
            out_ref[:, cols] = (
                jnp.dot(spread_near, got, preferred_element_type=jnp.float32)
                + from_far.astype(jnp.float32)
            ).astype(out_ref.dtype)
            return c

        lax.fori_loop(0, 5, gather, 0)

    block.wait_send()
    for h in range(2):
        sum_piece(h).wait_send()

    def drain(k, carry):
        first(k).wait_send()
        back(0, k).wait_send()
        back(1, k).wait_send()
        return carry

    lax.fori_loop(1, HALF, drain, 0)
    lax.fori_loop(HALF + 1, CHIPS, drain, 0)

    def drain_sibling(k, carry):
        share(k).wait_send()
        cross(k).wait_send()
        return carry

    lax.fori_loop(0, CHIPS, drain_sibling, 0)


def paired_body(tokens, routes, gate_quanta, gate_weight, up_weight, down_weight):
    tok_dev, width = tokens.shape
    experts = lax.axis_size("group")
    cap = 4 * tok_dev * routes.shape[1] // (3 * experts)
    hid = gate_weight.shape[2]
    bf, f32 = jnp.bfloat16, jnp.float32
    dma = pltpu.SemaphoreType.DMA
    vmem = pl.BlockSpec(memory_space=pltpu.VMEM)
    hbm = pl.BlockSpec(memory_space=pl.ANY)
    return pl.pallas_call(
        paired_kernel,
        out_shape=jax.ShapeDtypeStruct((tok_dev, width), bf),
        in_specs=[vmem, vmem, vmem, hbm, hbm, hbm],
        out_specs=vmem,
        scratch_shapes=[
            pltpu.VMEM((width, hid), bf),
            pltpu.VMEM((width, hid), bf),
            pltpu.VMEM((hid, width), bf),
            pltpu.VMEM((2, tok_dev, width + EXTRA), bf),
            pltpu.VMEM((2, 128, tok_dev), f32),
            pltpu.VMEM((CHIPS, cap, tok_dev), f32),
            pltpu.VMEM((CHIPS, cap, width + EXTRA), bf),
            pltpu.VMEM((CHIPS, 2, cap, width + EXTRA), bf),
            pltpu.VMEM((4 * cap, hid), bf),
            pltpu.VMEM((4 * cap, 128), f32),
            pltpu.VMEM((CHIPS, 2, cap, width), bf),
            pltpu.VMEM((CHIPS, cap, width), bf),
            pltpu.VMEM((CHIPS, cap, width), bf),
            pltpu.VMEM((CHIPS, cap, width), bf),
            pltpu.VMEM((2, tok_dev, width // 2), bf),
            pltpu.VMEM((2, tok_dev, width // 2), bf),
            dma((3,)),
            dma((1,)), dma((1,)), dma((2,)), dma((2,)),
        ] + [dma((CHIPS,))] * 6 + [dma((2, CHIPS))] * 2,
        compiler_params=pltpu.CompilerParams(
            collective_id=0, has_side_effects=True, vmem_limit_bytes=52 * 1024 * 1024
        ),
        cost_estimate=pl.CostEstimate(
            flops=6 * 16 * cap * width * hid, bytes_accessed=6 * width * hid, transcendentals=0
        ),
    )(tokens, routes.T, gate_quanta.T, gate_weight, up_weight, down_weight)


def expert_apply(received, gate_weight, up_weight, down_weight):
    senders = received.shape[0]
    slots_here = received.shape[1]
    inputs = received.reshape(senders * slots_here, received.shape[2])
    gate_part = jnp.dot(inputs, gate_weight[0], preferred_element_type=jnp.float32)
    up_part = jnp.dot(inputs, up_weight[0], preferred_element_type=jnp.float32)
    activ = (jax.nn.silu(gate_part) * up_part).astype(jnp.bfloat16)
    produced = jnp.dot(activ, down_weight[0], preferred_element_type=jnp.float32).astype(
        jnp.bfloat16
    )
    return produced.reshape(senders, slots_here, produced.shape[1])


def body(tokens, routes, gate_quanta, gate_weight, up_weight, down_weight):
    experts = lax.axis_size("group")
    tok_dev = tokens.shape[0]
    width = tokens.shape[1]
    topk = routes.shape[1]
    capacity = 4 * tok_dev * topk // (3 * experts)
    expert_ids = jnp.arange(experts, dtype=jnp.int32)
    matches = routes[:, :, None] == expert_ids[None, None, :]
    picked = jnp.sum(matches.astype(jnp.int32), axis=1)
    weight_quanta = jnp.sum(jnp.where(matches, gate_quanta[:, :, None], 0), axis=1)
    ranking = jnp.cumsum(picked, axis=0) - picked
    slot_of = jnp.where((picked == 1) & (ranking < capacity), ranking, -1)
    contract = (((0,), (0,)), ((), ()))
    selector = slot_of.T[:, None, :] == jnp.arange(capacity, dtype=jnp.int32)[None, :, None]
    selector_float = selector.astype(jnp.float32)
    selector_bf = selector.astype(jnp.bfloat16).reshape(experts * capacity, tok_dev)
    outgoing = jnp.dot(selector_bf, tokens, preferred_element_type=jnp.float32).astype(jnp.bfloat16)
    outgoing = outgoing.reshape(experts, capacity, width)
    produced = expert_apply(
        lax.all_to_all(outgoing, "group", split_axis=0, concat_axis=0, tiled=True),
        gate_weight,
        up_weight,
        down_weight,
    )
    returned = lax.all_to_all(produced, "group", split_axis=0, concat_axis=0, tiled=True)
    upper_part = (weight_quanta // 256).astype(jnp.float32).T / 256.0
    lower_part = (weight_quanta % 256).astype(jnp.float32).T / 65536.0
    combine_upper = (
        (selector_float * upper_part[:, None, :])
        .astype(jnp.bfloat16)
        .reshape(experts * capacity, tok_dev)
    )
    combine_lower = (
        (selector_float * lower_part[:, None, :])
        .astype(jnp.bfloat16)
        .reshape(experts * capacity, tok_dev)
    )
    flat_rows = returned.reshape(experts * capacity, width)
    running = lax.dot_general(
        combine_upper, flat_rows, contract, preferred_element_type=jnp.float32
    )
    running = running + lax.dot_general(
        combine_lower, flat_rows, contract, preferred_element_type=jnp.float32
    )
    return running.astype(jnp.bfloat16)


def solution(mesh):
    placed = (
        P(("parts", "group"), None),
        P(("parts", "group"), None),
        P(("parts", "group"), None),
        P("group", None, None),
        P("group", None, None),
        P("group", None, None),
    )
    chosen = paired_body if mesh.shape["group"] == 2 * CHIPS else body
    return jax.shard_map(
        chosen, mesh=mesh, in_specs=placed, out_specs=P(("parts", "group"), None), check_vma=False
    )
```
